512 devices in a mesh: rows: 64 (over y, z), dims: 8 (over x, core).
Axes of the slice: x: 4, y: 4, z: 16, core: 2. Of those that a mesh axis runs over, the one named last changes fastest.
Arguments:
- vectors: bfloat16 [262144, 1024], P('rows', 'dims'), may hold values from -16 to 16
- list_ids: int32 [262144], P('rows'), may hold values from 0 to 65535, as said below
- codes: int32 [262144, 64], P('rows', 'dims'), may hold values from 0 to 255
- old_centroids: float32 [65536, 1024], P('rows', 'dims'), may hold values from -6 to 6
- old_codebooks: float32 [256, 1024], P('rows', 'dims'), may hold values from -6 to 6
Outputs:
- new_centroids: float32 [65536, 1024], P('rows', 'dims')
- list_error: float32 [65536], P('rows')
- new_codebooks: float32 [256, 1024], P('rows', 'dims')
The draws below stay inside these ranges and needn't reach their ends.
Inputs may be any that keep to these rules, and one draw needn't show every extreme that they name: `list_ids`: among the vectors of one device, at most 128 name lists of any one aligned block of 1024 lists, and that bound is reached.
All inputs are finite; a program needn't handle non-finite values.
Results may differ from the reference program's by a relative error of at most 0.0003.
Values may be sent and summed in bfloat16 or wider, within the bound.
A program may use at most 64 MiB of HBM per device.

```python
import jax
import jax.numpy as jnp
from jax import lax

D = 1024
M = 64
K = 256
LIST_DEV = 1024
RDEV = 4096
NLIST = 65536
NROWS = 262144
CAP = 128
SUB = 16
PRIOR = 64


def draw_list_ids(key, part):
    owners = NLIST // LIST_DEV
    block_count = NROWS // RDEV
    slot_total = owners * CAP
    pool_key, rest_key = jax.random.split(jax.random.fold_in(key, 17))
    pool = jax.random.permutation(pool_key, owners)[:6].astype(jnp.int32)
    slot_owner = (jnp.arange(slot_total, dtype=jnp.int32) // CAP).astype(jnp.int32)

    def one_block(block_key):
        key_a, key_b, key_c, key_d = jax.random.split(block_key, 4)
        others = pool[1:][jax.random.permutation(key_a, 5)[:3]]
        hot_set = jnp.concatenate([pool[:1], others])
        is_hot = jnp.any(slot_owner[:, None] == hot_set[None, :], axis=1)
        score = jax.random.permutation(key_b, slot_total).astype(jnp.int32) - jnp.where(is_hot, slot_total, 0).astype(jnp.int32)
        order = jnp.argsort(score, stable=True)
        chosen = slot_owner[order[:RDEV]]
        chosen = jax.random.permutation(key_c, chosen)
        within = jax.random.randint(key_d, (RDEV,), 0, LIST_DEV, dtype=jnp.int32)
        return chosen * LIST_DEV + within
    block_keys = jax.random.split(rest_key, block_count)
    return jax.vmap(one_block)(block_keys).reshape(-1).astype(jnp.int32)


def draw_codes(key, part):
    code_key = jax.random.fold_in(key, 29)
    return jax.random.randint(code_key, (NROWS, M), 0, K, dtype=jnp.int32)


def draw_vectors(key, part):
    codes = draw_codes(key, part)
    own_key = jax.random.fold_in(key, 41)
    noise_key, table_key = jax.random.split(own_key)
    column = jnp.arange(D, dtype=jnp.float32) / D
    offsets = jax.random.uniform(table_key, (K, M, SUB), jnp.float32, -1.5, 1.5)
    picked = offsets[codes, jnp.arange(M, dtype=jnp.int32)[None, :]].reshape(NROWS, D)
    noise = 0.7 * jax.random.truncated_normal(noise_key, -4.0, 4.0, (NROWS, D), jnp.float32)
    common = 1.0
    scale = jnp.exp(0.5 * column * jnp.log(3.0))
    return ((common + picked + noise) * scale[None, :]).astype(jnp.bfloat16)


def block_levels(key, extent, cuts, least, largest):
    loudness = 1.0
    for dim, parts in cuts:
        steps = jax.random.uniform(jax.random.fold_in(jax.random.fold_in(key, 6), dim), (parts,), jnp.float32, least / len(cuts), largest / len(cuts))
        loudness = loudness * jnp.repeat(jnp.exp(steps), extent[dim] // parts).reshape((-1,) + (1,) * (len(extent) - 1 - dim))
    return loudness


def scatter_about(key, shape, scale, limit, cuts=(), kind=jnp.bfloat16):
    gain = block_levels(key, shape, cuts, -0.22, 0.18) if cuts else 1.0
    drawn = jax.random.normal(key, shape, jnp.float32) * scale * gain
    return jnp.minimum(jnp.maximum(drawn, -limit), limit).astype(kind)


def setup_inputs(seed: int = 0) -> dict:
    streams_of = jax.random.split(jax.random.key(seed), 6)
    return {
        "vectors": draw_vectors(jax.random.fold_in(streams_of[5], 71), 0),
        "list_ids": draw_list_ids(jax.random.fold_in(streams_of[5], 71), 0),
        "codes": draw_codes(jax.random.fold_in(streams_of[5], 71), 0),
        "old_centroids": scatter_about(streams_of[3], (NLIST, D), 1.0, 6.0, ((0, 64), (1, 8)), jnp.float32),
        "old_codebooks": scatter_about(streams_of[4], (K, D), 1.0, 6.0, ((0, 64), (1, 8)), jnp.float32),
    }


def reference(vectors, list_ids, codes, old_centroids, old_codebooks):
    as_float = vectors.astype(jnp.float32)
    ones_rows = jnp.ones(list_ids.shape, jnp.float32)
    list_sums = jax.ops.segment_sum(as_float, list_ids, num_segments=NLIST)
    list_counts = jax.ops.segment_sum(ones_rows, list_ids, num_segments=NLIST)
    new_centroids = (list_sums + old_centroids) / (list_counts[:, None] + 1.0)
    difference = as_float - new_centroids[list_ids]
    square = jnp.sum(difference * difference, axis=1)
    list_error = jax.ops.segment_sum(square, list_ids, num_segments=NLIST) / (list_counts + 1.0)
    residual = difference.astype(jnp.bfloat16)
    residual_split = residual.astype(jnp.float32).reshape(NROWS, M, SUB)

    def per_space(subspace):
        part_rows = lax.dynamic_index_in_dim(residual_split, subspace, 1, keepdims=False)
        labels = lax.dynamic_index_in_dim(codes, subspace, 1, keepdims=False)
        return (jax.ops.segment_sum(part_rows, labels, num_segments=K),
                jax.ops.segment_sum(ones_rows, labels, num_segments=K))

    code_sums, code_counts = lax.map(per_space, jnp.arange(M, dtype=jnp.int32))
    code_sums = jnp.transpose(code_sums, (1, 0, 2)).reshape(K, D)
    count_wide = jnp.repeat(code_counts.T, SUB, axis=1)
    prior_weight = PRIOR * 1.0
    new_codebooks = (code_sums + prior_weight * old_codebooks) / (count_wide + prior_weight)
    return new_centroids, list_error, new_codebooks
```

```python
import functools

import jax
import jax.numpy as jnp
from jax import lax
from jax.experimental import pallas as pl
from jax.experimental.pallas import tpu as pltpu
from jax.sharding import PartitionSpec as P

MESH = pl.DeviceIdType.MESH
LANES = 128
META = 16
VMEM_BYTES = 56 << 20
NN = (((1,), (0,)), ((), ()))
NT = (((1,), (1,)), ((), ()))


def dot(a, b, dims=NN):
    return lax.dot_general(a, b, dims, preferred_element_type=jnp.float32)


def id_value(local, bits=7):
    return ((1 << bits) + (local & ((1 << bits) - 1))) << (local >> bits)


def plan_kernel(owned, ids_ref, codes_ref, meta_ref, from_ref, wide):
    owners, slots = from_ref.shape
    count = ids_ref.shape[1]
    subs = codes_ref.shape[0]
    ids = ids_ref[...]
    shift = owned.bit_length() - 1
    owner = ids >> shift
    value = id_value(ids & (owned - 1)).astype(jnp.float32)
    mine = lax.broadcasted_iota(jnp.int32, (owners, count), 0) == owner
    hits = mine.astype(jnp.float32).astype(jnp.bfloat16)
    piece = min(512, count)
    before = (
        lax.broadcasted_iota(jnp.int32, (piece, piece), 0)
        < lax.broadcasted_iota(jnp.int32, (piece, piece), 1)
    ).astype(jnp.float32).astype(jnp.bfloat16)
    running = jnp.zeros((owners, 1), jnp.float32)
    ranks = []
    for c in range(count // piece):
        part = hits[:, c * piece : (c + 1) * piece]
        wide_part = part.astype(jnp.float32)
        earlier = dot(part, before) + running
        ranks.append(jnp.sum(earlier * wide_part, axis=0, keepdims=True))
        running = running + jnp.sum(wide_part, axis=1, keepdims=True)
    rank = jnp.concatenate(ranks, axis=1).astype(jnp.int32)
    placed = (lax.broadcasted_iota(jnp.int32, (slots, count), 0) == rank)
    placed = placed.astype(jnp.float32).astype(jnp.bfloat16)
    index = lax.broadcasted_iota(jnp.int32, (1, count), 1)

    def spread(row):
        return dot(jnp.where(mine, row, 0.0).astype(jnp.bfloat16), placed, NT)

    for m in range(subs):
        wide[:, m, :] = spread((codes_ref[m : m + 1, :] + 1).astype(jnp.float32))
    seen = spread(value)
    wide[:, subs, :] = seen
    for m in range(subs + 1, META):
        wide[:, m, :] = jnp.zeros((owners, slots), jnp.float32)
    high = spread((index >> 6).astype(jnp.float32))
    low = spread((index & 63).astype(jnp.float32))
    from_ref[...] = jnp.where(seen > 0.0, high * 64.0 + low, float(count)).astype(jnp.int32)
    meta_ref[...] = wide[...].astype(jnp.bfloat16)


def exchange_kernel(from_ref, vec_ref, meta_ref, recv_ref, rows, tmp, send, send_sem, recv_sem):
    owners, slots = from_ref.shape
    count = vec_ref.shape[0]
    me, slice_index = lax.axis_index("rows"), lax.axis_index("dims")

    barrier = pltpu.get_barrier_semaphore()

    @pl.loop(1, owners)
    def _(k):
        pl.semaphore_signal(
            barrier, inc=1, device_id=(lax.rem(me + k, owners), slice_index), device_id_type=MESH
        )

    rows[0:count, :] = vec_ref[...].astype(jnp.float32)
    rows[count:, :] = jnp.zeros((rows.shape[0] - count, LANES), jnp.float32)
    pl.semaphore_wait(barrier, owners - 1)

    def pack(d):
        @pl.loop(0, slots // 8)
        def _(q):
            for r in range(8):
                i = from_ref[d, q * 8 + r]
                tmp[pl.ds(q * 8 + r, 1), :] = rows[pl.ds(i, 1), :]

    def copy_to(d, slot, sem):
        return pltpu.make_async_remote_copy(
            src_ref=send.at[d],
            dst_ref=recv_ref.at[slot],
            send_sem=send_sem.at[d],
            recv_sem=recv_sem.at[sem],
            device_id=(d, slice_index),
            device_id_type=MESH,
        )

    @pl.loop(1, owners)
    def _(k):
        d = lax.rem(me + k, owners)
        pack(d)
        send[d, 0:slots, :] = tmp[...].astype(jnp.bfloat16)
        send[d, slots:, :] = meta_ref[d]
        copy_to(d, me, me).start()

    pack(me)
    recv_ref[me, 0:slots, :] = tmp[...].astype(jnp.bfloat16)
    recv_ref[me, slots:, :] = meta_ref[me]

    @pl.loop(1, owners)
    def _(k):
        d = lax.rem(me + k, owners)
        copy = copy_to(d, d, d)
        copy.wait_recv()
        copy.wait_send()


def owner_kernel(subs, recv_ref, old_ref, new_ref, sq_ref, csum_ref, ccnt_ref, acc, both, listcol, listrow, resid, c8):
    owners, block, _ = recv_ref.shape
    slots = block - META
    owned = old_ref.shape[0]
    codewords = csum_ref.shape[0]
    one, zero = jnp.bfloat16(1), jnp.bfloat16(0)
    ones = jnp.ones((slots, LANES), jnp.bfloat16)
    groups, lists = owned // 16, owned // LANES
    at = lax.broadcasted_iota(jnp.int32, (groups, 16, LANES), 0) * 16
    at = at + lax.broadcasted_iota(jnp.int32, (groups, 16, LANES), 1)
    listcol[...] = id_value(at).astype(jnp.float32).astype(jnp.bfloat16)
    at = lax.broadcasted_iota(jnp.int32, (lists, 16, LANES), 0) * LANES
    at = at + lax.broadcasted_iota(jnp.int32, (lists, 16, LANES), 2)
    listrow[...] = id_value(at).astype(jnp.float32).astype(jnp.bfloat16)

    def meta_row(b, m):
        return recv_ref[b, slots:, :].astype(jnp.float32)[m : m + 1, :]

    per = min(8, owners)
    acc[...] = jnp.zeros_like(acc)

    @pl.loop(0, owners // per)
    def _(g):
        hots, xs = [], []
        for j in range(per):
            b = g * per + j
            v = jnp.broadcast_to(meta_row(b, subs), (16, LANES)).astype(jnp.bfloat16)
            hit = listcol[...] == v[None]
            hots.append(jnp.where(hit, one, zero).reshape(owned, slots))
            xs.append(jnp.concatenate([recv_ref[b, 0:slots, :], ones], axis=1))
        acc[...] += dot(jnp.concatenate(hots, axis=1), jnp.concatenate(xs, axis=0))

    fresh = (acc[:, :LANES] + old_ref[...]) / (acc[:, LANES:] + 1.0)
    new_ref[...] = fresh
    top = fresh.astype(jnp.bfloat16)
    both[:, :LANES] = top
    both[:, LANES:] = (fresh - top.astype(jnp.float32)).astype(jnp.bfloat16)

    sq_ref[...] = jnp.zeros_like(sq_ref)
    eye = lax.broadcasted_iota(jnp.int32, (slots, LANES), 0) == lax.broadcasted_iota(
        jnp.int32, (slots, LANES), 1
    )
    kind = lax.broadcasted_iota(jnp.int32, (16, 2 * LANES), 0)

    @pl.loop(0, owners // 2)
    def _(g):
        hots, xs = [], []
        for j in range(2):
            b = g * 2 + j
            v = jnp.broadcast_to(meta_row(b, subs), (slots, LANES)).T.astype(jnp.bfloat16)
            v = v.reshape(slots // 16, 16, LANES)
            hots.append(
                jnp.concatenate(
                    [
                        jnp.where(v == listrow[t][None], one, zero).reshape(slots, LANES)
                        for t in range(lists)
                    ],
                    axis=1,
                )
            )
            xs.append(recv_ref[b, 0:slots, :].astype(jnp.float32))
        hot = jnp.concatenate(hots, axis=0)
        looked = dot(hot, both[...])
        diff = jnp.concatenate(xs, axis=0) - (looked[:, :LANES] + looked[:, LANES:])
        narrow = diff.astype(jnp.bfloat16)
        square = jnp.sum(diff * diff, axis=1, keepdims=True)
        rows = []
        for j in range(2):
            resid[g * 2 + j] = narrow[j * slots : (j + 1) * slots, :]
            rows.append(
                jnp.sum(jnp.where(eye, square[j * slots : (j + 1) * slots], 0.0), axis=0, keepdims=True)
            )
        square = jnp.concatenate(rows, axis=1)
        first = square.astype(jnp.bfloat16).astype(jnp.float32)
        second = (square - first).astype(jnp.bfloat16).astype(jnp.float32)
        third = square - first - second
        parts = jnp.where(kind == 0, first, jnp.where(kind == 1, second, jnp.where(kind == 2, third, 1.0)))
        sq_ref[...] += dot(parts.astype(jnp.bfloat16), hot)

    c8[...] = jnp.zeros_like(c8)
    words = lax.broadcasted_iota(jnp.int32, (codewords // 16, 16, LANES), 0) * 16
    words = words + lax.broadcasted_iota(jnp.int32, (codewords // 16, 16, LANES), 1) + 1
    words = words.astype(jnp.float32).astype(jnp.bfloat16)

    @pl.loop(0, owners // per)
    def _(g):
        right = jnp.concatenate(
            [jnp.concatenate([resid[g * per + j], ones], axis=1) for j in range(per)], axis=0
        )
        for m in range(subs):
            hots = []
            for j in range(per):
                v = jnp.broadcast_to(meta_row(g * per + j, m), (16, LANES)).astype(jnp.bfloat16)
                hots.append(jnp.where(words == v[None], one, zero).reshape(codewords, slots))
            c8[m] += dot(jnp.concatenate(hots, axis=1), right)

    sub = lax.broadcasted_iota(jnp.int32, (codewords, LANES), 1) // (LANES // subs)
    sums = jnp.zeros((codewords, LANES), jnp.float32)
    counts = jnp.zeros((codewords, LANES), jnp.float32)
    for m in range(subs):
        sums = jnp.where(sub == m, c8[m, :, :LANES], sums)
        counts = jnp.where(sub == m, c8[m, :, LANES:], counts)
    csum_ref[...] = sums
    ccnt_ref[...] = counts


def reduce_kernel(prior, share_ref, part_ref, books_ref, count_ref, new_ref, error_ref, shares, parts, ssem, rsem, ssem2, rsem2):
    owners, height, _ = share_ref.shape
    slices = parts.shape[0]
    mine = height // 2
    me, slice_index = lax.axis_index("rows"), lax.axis_index("dims")
    barrier = pltpu.get_barrier_semaphore()

    @pl.loop(1, owners)
    def _(k):
        pl.semaphore_signal(
            barrier, inc=1, device_id=(lax.rem(me + k, owners), slice_index), device_id_type=MESH
        )

    @pl.loop(1, slices)
    def _(k):
        pl.semaphore_signal(
            barrier, inc=1, device_id=(me, lax.rem(slice_index + k, slices)), device_id_type=MESH
        )

    pl.semaphore_wait(barrier, owners + slices - 2)

    def share_copy(d, slot):
        return pltpu.make_async_remote_copy(
            src_ref=share_ref.at[d],
            dst_ref=shares.at[slot],
            send_sem=ssem.at[d],
            recv_sem=rsem.at[slot],
            device_id=(d, slice_index),
            device_id_type=MESH,
        )

    def part_copy(d, slot):
        return pltpu.make_async_remote_copy(
            src_ref=part_ref,
            dst_ref=parts.at[slot],
            send_sem=ssem2.at[d],
            recv_sem=rsem2.at[slot],
            device_id=(me, d),
            device_id_type=MESH,
        )

    @pl.loop(1, slices)
    def _(k):
        part_copy(lax.rem(slice_index + k, slices), slice_index).start()

    @pl.loop(1, owners)
    def _(k):
        share_copy(lax.rem(me + k, owners), me).start()

    parts[slice_index] = part_ref[...]
    shares[me] = share_ref[me]

    @pl.loop(1, slices)
    def _(k):
        d = lax.rem(slice_index + k, slices)
        copy = part_copy(d, d)
        copy.wait_recv()
        copy.wait_send()

    @pl.loop(1, owners)
    def _(k):
        d = lax.rem(me + k, owners)
        copy = share_copy(d, d)
        copy.wait_recv()
        copy.wait_send()

    error_ref[...] = jnp.sum(parts[...], axis=0) / (count_ref[...] + 1.0)
    total = jnp.sum(shares[...], axis=0)
    new_ref[...] = (total[:mine] + prior * books_ref[...]) / (total[mine:] + prior)


def vmem_spec():
    return pl.BlockSpec(memory_space=pltpu.VMEM)


def body(vectors, list_ids, codes, old_centroids, old_codebooks):
    owners = lax.axis_size("rows")
    slices = lax.axis_size("dims")
    count = vectors.shape[0]
    owned = old_centroids.shape[0]
    subs = codes.shape[1]
    mine = old_codebooks.shape[0]
    codewords = mine * owners
    slots = 2 * count // owners
    block = slots + META
    f32, bf16 = jnp.float32, jnp.bfloat16
    meta, source = pl.pallas_call(
        functools.partial(plan_kernel, owned),
        out_shape=(
            jax.ShapeDtypeStruct((owners, META, LANES), bf16),
            jax.ShapeDtypeStruct((owners, slots), jnp.int32),
        ),
        in_specs=[vmem_spec()] * 2,
        out_specs=(vmem_spec(), vmem_spec()),
        scratch_shapes=[pltpu.VMEM((owners, META, LANES), f32)],
        compiler_params=pltpu.CompilerParams(vmem_limit_bytes=VMEM_BYTES),
        name="plan",
    )(list_ids.reshape(1, count), codes.T)
    received = pl.pallas_call(
        exchange_kernel,
        out_shape=jax.ShapeDtypeStruct((owners, block, LANES), bf16),
        in_specs=[pl.BlockSpec(memory_space=pltpu.SMEM), vmem_spec(), vmem_spec()],
        out_specs=vmem_spec(),
        scratch_shapes=[
            pltpu.VMEM((count + 8, LANES), f32),
            pltpu.VMEM((slots, LANES), f32),
            pltpu.VMEM((owners, block, LANES), bf16),
            pltpu.SemaphoreType.DMA((owners,)),
            pltpu.SemaphoreType.DMA((owners,)),
        ],
        compiler_params=pltpu.CompilerParams(
            collective_id=0, has_side_effects=True, vmem_limit_bytes=VMEM_BYTES
        ),
        name="exchange",
    )(source, vectors, meta)
    fresh, squares, code_sums, code_counts = pl.pallas_call(
        functools.partial(owner_kernel, subs),
        out_shape=(
            jax.ShapeDtypeStruct((owned, LANES), f32),
            jax.ShapeDtypeStruct((16, owned), f32),
            jax.ShapeDtypeStruct((codewords, LANES), f32),
            jax.ShapeDtypeStruct((codewords, LANES), f32),
        ),
        in_specs=[vmem_spec()] * 2,
        out_specs=(vmem_spec(),) * 4,
        scratch_shapes=[
            pltpu.VMEM((owned, 2 * LANES), f32),
            pltpu.VMEM((owned, 2 * LANES), bf16),
            pltpu.VMEM((owned // 16, 16, LANES), bf16),
            pltpu.VMEM((owned // LANES, 16, LANES), bf16),
            pltpu.VMEM((owners, slots, LANES), bf16),
            pltpu.VMEM((subs, codewords, 2 * LANES), f32),
        ],
        compiler_params=pltpu.CompilerParams(vmem_limit_bytes=VMEM_BYTES),
        name="owner",
    )(received, old_centroids)
    part = (squares[0] + squares[1] + squares[2]).reshape(owned // LANES, LANES)
    counts = squares[3].reshape(owned // LANES, LANES)
    share = jnp.concatenate(
        [code_sums.reshape(owners, mine, LANES), code_counts.reshape(owners, mine, LANES)], axis=1
    )
    prior = count * owners // (16 * codewords) * 1.0
    books, errors = pl.pallas_call(
        functools.partial(reduce_kernel, prior),
        out_shape=(
            jax.ShapeDtypeStruct((mine, LANES), f32),
            jax.ShapeDtypeStruct((owned // LANES, LANES), f32),
        ),
        in_specs=[vmem_spec()] * 4,
        out_specs=(vmem_spec(), vmem_spec()),
        scratch_shapes=[
            pltpu.VMEM((owners, 2 * mine, LANES), f32),
            pltpu.VMEM((slices, owned // LANES, LANES), f32),
            pltpu.SemaphoreType.DMA((owners,)),
            pltpu.SemaphoreType.DMA((owners,)),
            pltpu.SemaphoreType.DMA((slices,)),
            pltpu.SemaphoreType.DMA((slices,)),
        ],
        compiler_params=pltpu.CompilerParams(
            collective_id=1, has_side_effects=True, vmem_limit_bytes=VMEM_BYTES
        ),
        name="reduce",
    )(share, part, old_codebooks, counts)
    return fresh, errors.reshape(owned), books


def solution(mesh):
    in_specs = (
        P("rows", "dims"),
        P("rows"),
        P("rows", "dims"),
        P("rows", "dims"),
        P("rows", "dims"),
    )
    out_specs = (P("rows", "dims"), P("rows"), P("rows", "dims"))
    return jax.shard_map(body, mesh=mesh, in_specs=in_specs, out_specs=out_specs, check_vma=False)
```

```python
import functools

import jax
import jax.numpy as jnp
from jax import lax
from jax.experimental import pallas as pl
from jax.experimental.pallas import tpu as pltpu
from jax.sharding import PartitionSpec as P

MESH = pl.DeviceIdType.MESH
LANES = 128
META = 16
VMEM_BYTES = 56 << 20
YS = 4
GROUP = 4
WIDE = 8
CHUNK = 16
NN = (((1,), (0,)), ((), ()))
NT = (((1,), (1,)), ((), ()))


def dot(a, b, dims=NN):
    return lax.dot_general(a, b, dims, preferred_element_type=jnp.float32)


def id_value(local, bits=7):
    return ((1 << bits) + (local & ((1 << bits) - 1))) << (local >> bits)


def plan_kernel(owned, ids_ref, codes_ref, meta_ref, from_ref, wide):
    owners, slots = from_ref.shape
    count = ids_ref.shape[1]
    subs = codes_ref.shape[0]
    ids = ids_ref[...]
    shift = owned.bit_length() - 1
    owner = ids >> shift
    value = id_value(ids & (owned - 1)).astype(jnp.float32)
    mine = lax.broadcasted_iota(jnp.int32, (owners, count), 0) == owner
    hits = mine.astype(jnp.float32).astype(jnp.bfloat16)
    piece = min(512, count)
    before = (
        lax.broadcasted_iota(jnp.int32, (piece, piece), 0)
        < lax.broadcasted_iota(jnp.int32, (piece, piece), 1)
    ).astype(jnp.float32).astype(jnp.bfloat16)
    running = jnp.zeros((owners, 1), jnp.float32)
    ranks = []
    for c in range(count // piece):
        part = hits[:, c * piece : (c + 1) * piece]
        wide_part = part.astype(jnp.float32)
        earlier = dot(part, before) + running
        ranks.append(jnp.sum(earlier * wide_part, axis=0, keepdims=True))
        running = running + jnp.sum(wide_part, axis=1, keepdims=True)
    rank = jnp.concatenate(ranks, axis=1).astype(jnp.int32)
    placed = (lax.broadcasted_iota(jnp.int32, (slots, count), 0) == rank)
    placed = placed.astype(jnp.float32).astype(jnp.bfloat16)
    index = lax.broadcasted_iota(jnp.int32, (1, count), 1)

    def spread(row):
        return dot(jnp.where(mine, row, 0.0).astype(jnp.bfloat16), placed, NT)

    for m in range(subs):
        wide[:, m, :] = spread((codes_ref[m : m + 1, :] + 1).astype(jnp.float32))
    seen = spread(value)
    wide[:, subs, :] = seen
    for m in range(subs + 1, META):
        wide[:, m, :] = jnp.zeros((owners, slots), jnp.float32)
    high = spread((index >> 6).astype(jnp.float32))
    low = spread((index & 63).astype(jnp.float32))
    from_ref[...] = jnp.where(seen > 0.0, high * 64.0 + low, float(count)).astype(jnp.int32)
    meta_ref[...] = wide[...].astype(jnp.bfloat16)


def constants(listcol, listrow):
    groups, lists = listcol.shape[0], listrow.shape[0]
    at = lax.broadcasted_iota(jnp.int32, (groups, 16, LANES), 0) * 16
    at = at + lax.broadcasted_iota(jnp.int32, (groups, 16, LANES), 1)
    listcol[...] = id_value(at).astype(jnp.float32).astype(jnp.bfloat16)
    at = lax.broadcasted_iota(jnp.int32, (lists, 16, LANES), 0) * LANES
    at = at + lax.broadcasted_iota(jnp.int32, (lists, 16, LANES), 2)
    listrow[...] = id_value(at).astype(jnp.float32).astype(jnp.bfloat16)


def one_hot(hit):
    made = jnp.where(hit, jnp.bfloat16(1), jnp.bfloat16(0))
    return made.reshape(made.shape[0] * made.shape[1], made.shape[2])


def absorb(g, subs, recv, acc, hot, listcol, listrow):
    slots = recv.shape[1] - META
    lists = listrow.shape[0]
    hots, xs = [], []
    ones = jnp.ones((slots, LANES), jnp.bfloat16)
    for j in range(GROUP):
        b = g * GROUP + j
        v = recv[b, slots:, :].astype(jnp.float32)[subs : subs + 1, :]
        row = jnp.broadcast_to(v, (16, LANES)).astype(jnp.bfloat16)
        hots.append(one_hot(listcol[...] == row[None]))
        xs.append(jnp.concatenate([recv[b, 0:slots, :], ones], axis=1))
        column = jnp.broadcast_to(v, (slots, LANES)).T.astype(jnp.bfloat16)
        column = column.reshape(slots // 16, 16, LANES)
        start = pl.multiple_of(b * slots, slots)
        for t in range(lists):
            hot[pl.ds(start, slots), t * LANES : (t + 1) * LANES] = one_hot(column == listrow[t][None])
    acc[...] += dot(jnp.concatenate(hots, axis=1), jnp.concatenate(xs, axis=0))


def refit(old_ref, new_ref, acc, both):
    fresh = (acc[:, :LANES] + old_ref[...]) / (acc[:, LANES:] + 1.0)
    new_ref[...] = fresh
    top = fresh.astype(jnp.bfloat16)
    both[:, :LANES] = top
    both[:, LANES:] = (fresh - top.astype(jnp.float32)).astype(jnp.bfloat16)


def residuals(recv, hot, both, resid, squares):
    owners, slots = recv.shape[0], recv.shape[1] - META
    per = min(WIDE, owners)
    wide = per * slots

    @pl.loop(0, owners // per)
    def _(g):
        start = pl.multiple_of(g * wide, wide)
        looked = dot(hot[pl.ds(start, wide), :], both[...])
        x = jnp.concatenate([recv[g * per + j, 0:slots, :] for j in range(per)], axis=0)
        diff = x.astype(jnp.float32) - (looked[:, :LANES] + looked[:, LANES:])
        resid[pl.ds(start, wide), :] = diff.astype(jnp.bfloat16)
        square = diff * diff
        top = square.astype(jnp.bfloat16)
        squares[pl.ds(start, wide), :LANES] = top
        squares[pl.ds(start, wide), LANES:] = (square - top.astype(jnp.float32)).astype(jnp.bfloat16)


def code_sums(subs, recv, resid, c8):
    owners, slots = recv.shape[0], recv.shape[1] - META
    codewords = c8.shape[1]
    per = min(CHUNK, owners)
    ones = jnp.ones((per * slots, LANES), jnp.bfloat16)
    words = lax.broadcasted_iota(jnp.int32, (codewords // 16, 16, LANES), 0) * 16
    words = words + lax.broadcasted_iota(jnp.int32, (codewords // 16, 16, LANES), 1) + 1
    words = words.astype(jnp.float32).astype(jnp.bfloat16)
    c8[...] = jnp.zeros_like(c8)

    @pl.loop(0, owners // per)
    def _(g):
        start = pl.multiple_of(g * per * slots, per * slots)
        right = jnp.concatenate([resid[pl.ds(start, per * slots), :], ones], axis=1)
        for m in range(subs):
            hots = []
            for j in range(per):
                v = recv[g * per + j, slots:, :].astype(jnp.float32)[m : m + 1, :]
                row = jnp.broadcast_to(v, (16, LANES)).astype(jnp.bfloat16)
                hots.append(one_hot(words == row[None]))
            c8[m] += dot(jnp.concatenate(hots, axis=1), right)


def list_squares(hot, squares, parts, total):
    count = squares.shape[0]
    wide = min(2048, count)
    ones = jnp.ones((16, 2 * LANES), jnp.bfloat16)
    kind = lax.broadcasted_iota(jnp.int32, (16, wide), 0)

    @pl.loop(0, count // wide)
    def _(g):
        start = pl.multiple_of(g * wide, wide)
        row = dot(ones, squares[pl.ds(start, wide), :], NT)
        first = row.astype(jnp.bfloat16).astype(jnp.float32)
        second = (row - first).astype(jnp.bfloat16).astype(jnp.float32)
        third = row - first - second
        row = jnp.where(kind == 0, first, jnp.where(kind == 1, second, jnp.where(kind == 2, third, 1.0)))
        parts[g] = row.astype(jnp.bfloat16)

    total[...] = jnp.zeros_like(total)

    @pl.loop(0, count // wide)
    def _(g):
        start = pl.multiple_of(g * wide, wide)
        total[...] += dot(parts[g], hot[pl.ds(start, wide), :])


def gather_shares(subs, mine, c8, sums, counts, share):
    codewords = c8.shape[1]
    sub = lax.broadcasted_iota(jnp.int32, (codewords, LANES), 1) // (LANES // subs)
    s = jnp.zeros((codewords, LANES), jnp.float32)
    n = jnp.zeros((codewords, LANES), jnp.float32)
    for m in range(subs):
        s = jnp.where(sub == m, c8[m, :, :LANES], s)
        n = jnp.where(sub == m, c8[m, :, LANES:], n)
    sums[...] = s
    counts[...] = n
    for d in range(codewords // mine):
        share[d // share.shape[1], d % share.shape[1], 0:mine, :] = sums[d * mine : (d + 1) * mine, :]
        share[d // share.shape[1], d % share.shape[1], mine:, :] = counts[d * mine : (d + 1) * mine, :]


def main_kernel(
    subs, prior, from_ref, vec_ref, meta_ref, old_ref, books_ref, new_ref, error_ref, words_ref,
    rows, tmp, send, recv, acc, both, listcol, listrow, hot, resid, squares, parts, total, c8,
    sums, counts, share, near, passed, far, part, others,
    send_sem, recv_sem, ysend, yrecv, zsend, zrecv, psend, precv,
):
    owners, slots = from_ref.shape
    count = vec_ref.shape[0]
    slices = others.shape[0]
    mine = books_ref.shape[0]
    ys, zs = share.shape[0], share.shape[1]
    me, slice_index = lax.axis_index("rows"), lax.axis_index("dims")
    y, z = me // zs, lax.rem(me, zs)

    barrier = pltpu.get_barrier_semaphore()

    @pl.loop(1, owners)
    def _(k):
        pl.semaphore_signal(
            barrier, inc=1, device_id=(lax.rem(me + k, owners), slice_index), device_id_type=MESH
        )

    @pl.loop(1, slices)
    def _(k):
        pl.semaphore_signal(
            barrier, inc=1, device_id=(me, lax.rem(slice_index + k, slices)), device_id_type=MESH
        )

    rows[0:count, :] = vec_ref[...].astype(jnp.float32)
    rows[count:, :] = jnp.zeros((rows.shape[0] - count, LANES), jnp.float32)
    constants(listcol, listrow)
    acc[...] = jnp.zeros_like(acc)
    pl.semaphore_wait(barrier, owners + slices - 2)

    def pack(d):
        @pl.loop(0, slots // 8)
        def _(q):
            for r in range(8):
                i = from_ref[d, q * 8 + r]
                tmp[pl.ds(q * 8 + r, 1), :] = rows[pl.ds(i, 1), :]

    def copy_to(k):
        d = lax.rem(me + k, owners)
        return pltpu.make_async_remote_copy(
            src_ref=send.at[k],
            dst_ref=recv.at[k],
            send_sem=send_sem.at[k],
            recv_sem=recv_sem.at[k],
            device_id=(d, slice_index),
            device_id_type=MESH,
        )

    @pl.loop(1, owners)
    def _(k):
        d = lax.rem(me + k, owners)
        pack(d)
        send[k, 0:slots, :] = tmp[...].astype(jnp.bfloat16)
        send[k, slots:, :] = meta_ref[d]
        copy_to(k).start()

    pack(me)
    recv[0, 0:slots, :] = tmp[...].astype(jnp.bfloat16)
    recv[0, slots:, :] = meta_ref[me]

    @pl.loop(0, owners // GROUP)
    def _(g):
        for j in range(GROUP):
            k = g * GROUP + j

            @pl.when(k > 0)
            def _():
                copy_to(k).wait_recv()

        absorb(g, subs, recv, acc, hot, listcol, listrow)

    refit(old_ref, new_ref, acc, both)
    residuals(recv, hot, both, resid, squares)
    code_sums(subs, recv, resid, c8)
    gather_shares(subs, mine, c8, sums, counts, share)

    def y_copy(k):
        to = lax.rem(y + k, ys)
        return pltpu.make_async_remote_copy(
            src_ref=share.at[to],
            dst_ref=near.at[k],
            send_sem=ysend.at[k],
            recv_sem=yrecv.at[k],
            device_id=(to * zs + z, slice_index),
            device_id_type=MESH,
        )

    def z_copy(k):
        to = lax.rem(z + k, zs)
        return pltpu.make_async_remote_copy(
            src_ref=passed.at[to],
            dst_ref=far.at[k],
            send_sem=zsend.at[k],
            recv_sem=zrecv.at[k],
            device_id=(y * zs + to, slice_index),
            device_id_type=MESH,
        )

    def part_copy(k):
        return pltpu.make_async_remote_copy(
            src_ref=part,
            dst_ref=others.at[k],
            send_sem=psend.at[k],
            recv_sem=precv.at[k],
            device_id=(me, lax.rem(slice_index + k, slices)),
            device_id_type=MESH,
        )

    for k in range(1, ys):
        y_copy(k).start()
    list_squares(hot, squares, parts, total)
    for t in range(part.shape[0]):
        at = slice(t * LANES, (t + 1) * LANES)
        part[t : t + 1, :] = total[0:1, at] + total[1:2, at] + total[2:3, at]

    @pl.loop(1, slices)
    def _(k):
        part_copy(k).start()

    near[0] = share[y]
    for k in range(1, ys):
        y_copy(k).wait_recv()
    passed[...] = jnp.sum(near[...], axis=0)

    @pl.loop(1, zs)
    def _(k):
        z_copy(k).start()

    far[0] = passed[z]
    others[0] = part[...]

    @pl.loop(1, slices)
    def _(k):
        part_copy(k).wait_recv()

    spread = jnp.sum(others[...], axis=0)
    for t in range(part.shape[0]):
        error_ref[t : t + 1, :] = spread[t : t + 1, :] / (total[3:4, t * LANES : (t + 1) * LANES] + 1.0)

    @pl.loop(1, zs)
    def _(k):
        z_copy(k).wait_recv()

    whole = jnp.sum(far[...], axis=0)
    words_ref[...] = (whole[:mine] + prior * books_ref[...]) / (whole[mine:] + prior)

    @pl.loop(1, owners)
    def _(k):
        copy_to(k).wait_send()

    for k in range(1, ys):
        y_copy(k).wait_send()

    @pl.loop(1, zs)
    def _(k):
        z_copy(k).wait_send()

    @pl.loop(1, slices)
    def _(k):
        part_copy(k).wait_send()


def vmem_spec():
    return pl.BlockSpec(memory_space=pltpu.VMEM)


def body(vectors, list_ids, codes, old_centroids, old_codebooks):
    owners = lax.axis_size("rows")
    slices = lax.axis_size("dims")
    count = vectors.shape[0]
    owned = old_centroids.shape[0]
    subs = codes.shape[1]
    mine = old_codebooks.shape[0]
    codewords = mine * owners
    slots = 2 * count // owners
    block = slots + META
    f32, bf16 = jnp.float32, jnp.bfloat16
    meta, source = pl.pallas_call(
        functools.partial(plan_kernel, owned),
        out_shape=(
            jax.ShapeDtypeStruct((owners, META, LANES), bf16),
            jax.ShapeDtypeStruct((owners, slots), jnp.int32),
        ),
        in_specs=[vmem_spec()] * 2,
        out_specs=(vmem_spec(), vmem_spec()),
        scratch_shapes=[pltpu.VMEM((owners, META, LANES), f32)],
        compiler_params=pltpu.CompilerParams(vmem_limit_bytes=VMEM_BYTES),
        name="plan",
    )(list_ids.reshape(1, count), codes.T)
    prior = count * owners // (16 * codewords) * 1.0
    zs = owners // YS
    vmem, dma = pltpu.VMEM, pltpu.SemaphoreType.DMA
    wide = min(2048, owners * slots)
    fresh, errors, books = pl.pallas_call(
        functools.partial(main_kernel, subs, prior),
        out_shape=(
            jax.ShapeDtypeStruct((owned, LANES), f32),
            jax.ShapeDtypeStruct((owned // LANES, LANES), f32),
            jax.ShapeDtypeStruct((mine, LANES), f32),
        ),
        in_specs=[pl.BlockSpec(memory_space=pltpu.SMEM)] + [vmem_spec()] * 4,
        out_specs=(vmem_spec(),) * 3,
        scratch_shapes=[
            vmem((count + 8, LANES), f32),
            vmem((slots, LANES), f32),
            vmem((owners, block, LANES), bf16),
            vmem((owners, block, LANES), bf16),
            vmem((owned, 2 * LANES), f32),
            vmem((owned, 2 * LANES), bf16),
            vmem((owned // 16, 16, LANES), bf16),
            vmem((owned // LANES, 16, LANES), bf16),
            vmem((owners * slots, owned), bf16),
            vmem((owners * slots, LANES), bf16),
            vmem((owners * slots, 2 * LANES), bf16),
            vmem((owners * slots // wide, 16, wide), bf16),
            vmem((16, owned), f32),
            vmem((subs, codewords, 2 * LANES), f32),
            vmem((codewords, LANES), f32),
            vmem((codewords, LANES), f32),
            vmem((YS, zs, 2 * mine, LANES), f32),
            vmem((YS, zs, 2 * mine, LANES), f32),
            vmem((zs, 2 * mine, LANES), f32),
            vmem((zs, 2 * mine, LANES), f32),
            vmem((owned // LANES, LANES), f32),
            vmem((slices, owned // LANES, LANES), f32),
            dma((owners,)),
            dma((owners,)),
            dma((YS,)),
            dma((YS,)),
            dma((zs,)),
            dma((zs,)),
            dma((slices,)),
            dma((slices,)),
        ],
        compiler_params=pltpu.CompilerParams(
            collective_id=0, has_side_effects=True, vmem_limit_bytes=VMEM_BYTES
        ),
        name="main",
    )(source, vectors, meta, old_centroids, old_codebooks)
    return fresh, errors.reshape(owned), books


def solution(mesh):
    in_specs = (
        P("rows", "dims"),
        P("rows"),
        P("rows", "dims"),
        P("rows", "dims"),
        P("rows", "dims"),
    )
    out_specs = (P("rows", "dims"), P("rows"), P("rows", "dims"))
    return jax.shard_map(body, mesh=mesh, in_specs=in_specs, out_specs=out_specs, check_vma=False)
```

```python
import functools

import jax
import jax.numpy as jnp
from jax import lax
from jax.experimental import pallas as pl
from jax.experimental.pallas import tpu as pltpu
from jax.sharding import PartitionSpec as P

MESH = pl.DeviceIdType.MESH
LANES = 128
META = 16
VMEM_BYTES = 56 << 20
YS = 4
GROUP = 4
WIDE = 8
NEAR = 80
SPILL = 224
SPILL_META = 2 * META
CHUNK = 16
NN = (((1,), (0,)), ((), ()))
NT = (((1,), (1,)), ((), ()))


def dot(a, b, dims=NN):
    return lax.dot_general(a, b, dims, preferred_element_type=jnp.float32)


def id_value(local, bits=7):
    return ((1 << bits) + (local & ((1 << bits) - 1))) << (local >> bits)


def plan_kernel(owned, ids_ref, codes_ref, meta_ref, from_ref, wide):
    owners, slots = from_ref.shape
    count = ids_ref.shape[1]
    subs = codes_ref.shape[0]
    ids = ids_ref[...]
    shift = owned.bit_length() - 1
    owner = ids >> shift
    value = id_value(ids & (owned - 1)).astype(jnp.float32)
    mine = lax.broadcasted_iota(jnp.int32, (owners, count), 0) == owner
    hits = mine.astype(jnp.float32).astype(jnp.bfloat16)
    piece = min(512, count)
    before = (
        lax.broadcasted_iota(jnp.int32, (piece, piece), 0)
        < lax.broadcasted_iota(jnp.int32, (piece, piece), 1)
    ).astype(jnp.float32).astype(jnp.bfloat16)
    running = jnp.zeros((owners, 1), jnp.float32)
    ranks = []
    for c in range(count // piece):
        part = hits[:, c * piece : (c + 1) * piece]
        wide_part = part.astype(jnp.float32)
        earlier = dot(part, before) + running
        ranks.append(jnp.sum(earlier * wide_part, axis=0, keepdims=True))
        running = running + jnp.sum(wide_part, axis=1, keepdims=True)
    rank = jnp.concatenate(ranks, axis=1).astype(jnp.int32)
    placed = (lax.broadcasted_iota(jnp.int32, (slots, count), 0) == rank)
    placed = placed.astype(jnp.float32).astype(jnp.bfloat16)
    index = lax.broadcasted_iota(jnp.int32, (1, count), 1)

    def spread(row):
        return dot(jnp.where(mine, row, 0.0).astype(jnp.bfloat16), placed, NT)

    for m in range(subs):
        wide[:, m, :] = spread((codes_ref[m : m + 1, :] + 1).astype(jnp.float32))
    seen = spread(value)
    wide[:, subs, :] = seen
    for m in range(subs + 1, META):
        wide[:, m, :] = jnp.zeros((owners, slots), jnp.float32)
    high = spread((index >> 6).astype(jnp.float32))
    low = spread((index & 63).astype(jnp.float32))
    from_ref[...] = jnp.where(seen > 0.0, high * 64.0 + low, float(count)).astype(jnp.int32)
    meta_ref[...] = wide[...].astype(jnp.bfloat16)


def split_plan_kernel(owned, ids_ref, codes_ref, meta_ref, from_ref, spill_meta_ref, spill_from_ref, wide):
    owners, slots = from_ref.shape
    count = ids_ref.shape[1]
    subs = codes_ref.shape[0]
    spill = spill_from_ref.shape[1]
    ids = ids_ref[...]
    shift = owned.bit_length() - 1
    owner = ids >> shift
    value = id_value(ids & (owned - 1)).astype(jnp.float32)
    mine = lax.broadcasted_iota(jnp.int32, (owners, count), 0) == owner
    hits = mine.astype(jnp.float32).astype(jnp.bfloat16)
    piece = min(512, count)
    before = (
        lax.broadcasted_iota(jnp.int32, (piece, piece), 0)
        < lax.broadcasted_iota(jnp.int32, (piece, piece), 1)
    ).astype(jnp.float32).astype(jnp.bfloat16)
    running = jnp.zeros((owners, 1), jnp.float32)
    ranks = []
    for c in range(count // piece):
        part = hits[:, c * piece : (c + 1) * piece]
        wide_part = part.astype(jnp.float32)
        earlier = dot(part, before) + running
        ranks.append(jnp.sum(earlier * wide_part, axis=0, keepdims=True))
        running = running + jnp.sum(wide_part, axis=1, keepdims=True)
    rank = jnp.concatenate(ranks, axis=1)
    beyond = jnp.broadcast_to(jnp.maximum(running - NEAR, 0.0), (owners, LANES))
    lower = (
        lax.broadcasted_iota(jnp.int32, (owners, owners), 0)
        > lax.broadcasted_iota(jnp.int32, (owners, owners), 1)
    ).astype(jnp.float32).astype(jnp.bfloat16)
    start = dot(lower, beyond.astype(jnp.bfloat16))
    total = jnp.sum(beyond, axis=0, keepdims=True)
    first = jnp.sum(jnp.where(mine, start[:, 0:1], 0.0), axis=0, keepdims=True)
    near = jnp.where(rank < NEAR, rank, -1.0).astype(jnp.int32)
    far = jnp.where(rank < NEAR, -1.0, first + rank - NEAR).astype(jnp.int32)
    placed = lax.broadcasted_iota(jnp.int32, (slots, count), 0) == near
    placed = placed.astype(jnp.float32).astype(jnp.bfloat16)
    spilled = lax.broadcasted_iota(jnp.int32, (spill, count), 0) == far
    spilled = spilled.astype(jnp.float32).astype(jnp.bfloat16)
    index = lax.broadcasted_iota(jnp.int32, (1, count), 1)
    upper_index = (index >> 6).astype(jnp.float32)
    lower_index = (index & 63).astype(jnp.float32)
    words = (codes_ref[...] + 1).astype(jnp.float32)

    def spread(row):
        return dot(jnp.where(mine, row, 0.0).astype(jnp.bfloat16), placed, NT)

    for m in range(subs):
        wide[:, m, :] = spread(words[m : m + 1, :])
    seen = spread(value)
    wide[:, subs, :] = seen
    wide[:, subs + 1, :] = start
    wide[:, subs + 2, :] = start + beyond
    wide[:, subs + 3, :] = jnp.broadcast_to(jnp.where(total > SPILL, 1.0, 0.0), (owners, LANES))
    for m in range(subs + 4, META):
        wide[:, m, :] = jnp.zeros((owners, slots), jnp.float32)
    high, low = spread(upper_index), spread(lower_index)
    from_ref[...] = jnp.where(seen > 0.0, high * 64.0 + low, float(count)).astype(jnp.int32)
    meta_ref[...] = wide[...].astype(jnp.bfloat16)
    row = lax.broadcasted_iota(jnp.int32, (META - subs, count), 0)
    more = jnp.where(row == 0, value, jnp.where(row == 1, upper_index, jnp.where(row == 2, lower_index, 0.0)))
    moved = dot(jnp.concatenate([words, more], axis=0).astype(jnp.bfloat16), spilled, NT)
    spill_from_ref[...] = jnp.where(
        moved[subs : subs + 1] > 0.0,
        moved[subs + 1 : subs + 2] * 64.0 + moved[subs + 2 : subs + 3],
        float(count),
    ).astype(jnp.int32)
    for t in range(spill // LANES):
        spill_meta_ref[t * META : (t + 1) * META, :] = moved[:, t * LANES : (t + 1) * LANES].astype(jnp.bfloat16)


def constants(listcol, listrow):
    groups, lists = listcol.shape[0], listrow.shape[0]
    at = lax.broadcasted_iota(jnp.int32, (groups, 16, LANES), 0) * 16
    at = at + lax.broadcasted_iota(jnp.int32, (groups, 16, LANES), 1)
    listcol[...] = id_value(at).astype(jnp.float32).astype(jnp.bfloat16)
    at = lax.broadcasted_iota(jnp.int32, (lists, 16, LANES), 0) * LANES
    at = at + lax.broadcasted_iota(jnp.int32, (lists, 16, LANES), 2)
    listrow[...] = id_value(at).astype(jnp.float32).astype(jnp.bfloat16)


def one_hot(hit):
    made = jnp.where(hit, jnp.bfloat16(1), jnp.bfloat16(0))
    return made.reshape(made.shape[0] * made.shape[1], made.shape[2])


def low_words(v):
    return v - jnp.where(v > 128.5, 128.0, 0.0)


def word_rows(count):
    words = lax.broadcasted_iota(jnp.int32, (count // 16, 16, LANES), 0) * 16
    words = words + lax.broadcasted_iota(jnp.int32, (count // 16, 16, LANES), 1) + 1
    return words.astype(jnp.float32).astype(jnp.bfloat16)


def absorb(g, subs, recv, acc, hot, listcol, listrow, upper, n8):
    slots = recv.shape[1] - META
    lists = listrow.shape[0]
    hots, xs = [], []
    ones = jnp.ones((slots, LANES), jnp.bfloat16)
    words = word_rows(n8.shape[1])
    metas = [recv[g * GROUP + j, slots:, :].astype(jnp.float32) for j in range(GROUP)]
    uppers = []
    for j in range(GROUP):
        b = g * GROUP + j
        v = metas[j][subs : subs + 1, :]
        row = jnp.broadcast_to(v, (16, LANES)).astype(jnp.bfloat16)
        hots.append(one_hot(listcol[...] == row[None]))
        xs.append(jnp.concatenate([recv[b, 0:slots, :], ones], axis=1))
        column = jnp.broadcast_to(v, (slots, LANES)).T.astype(jnp.bfloat16)
        column = column.reshape(slots // 16, 16, LANES)
        start = pl.multiple_of(b * slots, slots)
        for t in range(lists):
            hot[pl.ds(start, slots), t * LANES : (t + 1) * LANES] = one_hot(column == listrow[t][None])
        is_upper = jnp.where(metas[j] > 128.5, 1.0, 0.0)
        is_upper = jnp.concatenate(
            [jnp.broadcast_to(is_upper[m : m + 1, :], (LANES // subs, LANES)) for m in range(subs)], axis=0
        )
        is_upper = is_upper.T.astype(jnp.bfloat16)
        upper[pl.ds(start, slots), :] = is_upper
        uppers.append(jnp.concatenate([ones - is_upper, is_upper], axis=1))
    acc[...] += dot(jnp.concatenate(hots, axis=1), jnp.concatenate(xs, axis=0))
    halves = jnp.concatenate(uppers, axis=0)
    lows = [low_words(v) for v in metas]
    for m in range(subs):
        hots = []
        for j in range(GROUP):
            row = jnp.broadcast_to(lows[j][m : m + 1, :], (16, LANES)).astype(jnp.bfloat16)
            hots.append(one_hot(words == row[None]))
        n8[m] += dot(jnp.concatenate(hots, axis=1), halves)


def refit(old_ref, new_ref, acc, both):
    fresh = (acc[:, :LANES] + old_ref[...]) / (acc[:, LANES:] + 1.0)
    new_ref[...] = fresh
    top = fresh.astype(jnp.bfloat16)
    both[:, :LANES] = top
    both[:, LANES:] = (fresh - top.astype(jnp.float32)).astype(jnp.bfloat16)


def residuals(recv, hot, both, resid, squares):
    owners, slots = recv.shape[0], recv.shape[1] - META
    per = min(WIDE, owners)
    wide = per * slots

    @pl.loop(0, owners // per)
    def _(g):
        start = pl.multiple_of(g * wide, wide)
        looked = dot(hot[pl.ds(start, wide), :], both[...])
        x = jnp.concatenate([recv[g * per + j, 0:slots, :] for j in range(per)], axis=0)
        diff = x.astype(jnp.float32) - (looked[:, :LANES] + looked[:, LANES:])
        resid[pl.ds(start, wide), :] = diff.astype(jnp.bfloat16)
        square = diff * diff
        top = square.astype(jnp.bfloat16)
        squares[pl.ds(start, wide), :LANES] = top
        squares[pl.ds(start, wide), LANES:] = (square - top.astype(jnp.float32)).astype(jnp.bfloat16)


def code_sums(subs, recv, resid, upper, c8):
    owners, slots = recv.shape[0], recv.shape[1] - META
    per = min(CHUNK, owners)
    words = word_rows(c8.shape[1])
    c8[...] = jnp.zeros_like(c8)

    @pl.loop(0, owners // per)
    def _(g):
        start = pl.multiple_of(g * per * slots, per * slots)
        r = resid[pl.ds(start, per * slots), :]
        in_upper = r * upper[pl.ds(start, per * slots), :]
        right = jnp.concatenate([r - in_upper, in_upper], axis=1)
        lows = [low_words(recv[g * per + j, slots:, :].astype(jnp.float32)) for j in range(per)]
        for m in range(subs):
            hots = []
            for j in range(per):
                row = jnp.broadcast_to(lows[j][m : m + 1, :], (16, LANES)).astype(jnp.bfloat16)
                hots.append(one_hot(words == row[None]))
            c8[m] += dot(jnp.concatenate(hots, axis=1), right)


def list_squares(hot, squares, parts, total):
    count = squares.shape[0]
    wide = min(2048, count)
    ones = jnp.ones((16, 2 * LANES), jnp.bfloat16)
    kind = lax.broadcasted_iota(jnp.int32, (16, wide), 0)

    @pl.loop(0, count // wide)
    def _(g):
        start = pl.multiple_of(g * wide, wide)
        row = dot(ones, squares[pl.ds(start, wide), :], NT)
        first = row.astype(jnp.bfloat16).astype(jnp.float32)
        second = (row - first).astype(jnp.bfloat16).astype(jnp.float32)
        third = row - first - second
        row = jnp.where(kind == 0, first, jnp.where(kind == 1, second, jnp.where(kind == 2, third, 1.0)))
        parts[g] = row.astype(jnp.bfloat16)

    total[...] = jnp.zeros_like(total)

    @pl.loop(0, count // wide)
    def _(g):
        start = pl.multiple_of(g * wide, wide)
        total[...] += dot(parts[g], hot[pl.ds(start, wide), :])


def gather_shares(subs, mine, c8, n8, sums, counts, share):
    half = c8.shape[1]
    codewords = 2 * half
    sub = lax.broadcasted_iota(jnp.int32, (half, LANES), 1) // (LANES // subs)
    for taken, given in ((c8, sums), (n8, counts)):
        for h in range(2):
            s = jnp.zeros((half, LANES), jnp.float32)
            for m in range(subs):
                s = jnp.where(sub == m, taken[m, :, h * LANES : (h + 1) * LANES], s)
            given[h * half : (h + 1) * half, :] = s
    for d in range(codewords // mine):
        share[d // share.shape[1], d % share.shape[1], 0:mine, :] = sums[d * mine : (d + 1) * mine, :]
        share[d // share.shape[1], d % share.shape[1], mine:, :] = counts[d * mine : (d + 1) * mine, :]


def assemble(b, subs, land, block, recv, flag):
    slots = recv.shape[1] - META
    meta = land[b, NEAR:, :].astype(jnp.float32)
    begin, end = meta[subs + 1 : subs + 2, :], meta[subs + 2 : subs + 3, :]
    flag[...] = jnp.maximum(flag[...], meta[subs + 3 : subs + 4, :])
    slot = lax.broadcasted_iota(jnp.int32, (slots, LANES), 0)
    lane = lax.broadcasted_iota(jnp.int32, (slots, LANES), 1)
    halves = []
    for t in range(SPILL_META // META):
        at = (lane + t * LANES).astype(jnp.float32)
        wanted = jnp.where(slot >= NEAR, lane + t * LANES + NEAR - slot, -1).astype(jnp.float32)
        hit = jnp.logical_and(wanted == begin, at < end)
        halves.append(jnp.where(hit, 1.0, 0.0))
    pick = jnp.concatenate(halves, axis=1).astype(jnp.bfloat16)
    taken = dot(pick, block[...])
    recv[b, 0:NEAR, :] = land[b, 0:NEAR, :]
    recv[b, NEAR:slots, :] = taken[NEAR:, :].astype(jnp.bfloat16)
    labels = jnp.concatenate(
        [block[SPILL + t * META : SPILL + (t + 1) * META, :] for t in range(SPILL_META // META)], axis=1
    )
    keep = lax.broadcasted_iota(jnp.int32, (META, LANES), 1) < NEAR
    recv[b, slots:, :] = jnp.where(keep, meta, dot(labels, pick, NT)).astype(jnp.bfloat16)


def finish(
    subs, prior, old_ref, books_ref, new_ref, error_ref, words_ref, recv, acc, both, hot, resid, upper, squares, parts,
    total, c8, n8, sums, counts, share, near, passed, far, part, others, ysend, yrecv, zsend, zrecv, psend, precv,
):
    slices, mine = others.shape[0], books_ref.shape[0]
    ys, zs = share.shape[0], share.shape[1]
    me, slice_index = lax.axis_index("rows"), lax.axis_index("dims")
    y, z = me // zs, lax.rem(me, zs)
    refit(old_ref, new_ref, acc, both)
    residuals(recv, hot, both, resid, squares)
    code_sums(subs, recv, resid, upper, c8)
    gather_shares(subs, mine, c8, n8, sums, counts, share)

    def y_copy(k):
        to = lax.rem(y + k, ys)
        return pltpu.make_async_remote_copy(
            src_ref=share.at[to],
            dst_ref=near.at[k],
            send_sem=ysend.at[k],
            recv_sem=yrecv.at[k],
            device_id=(to * zs + z, slice_index),
            device_id_type=MESH,
        )

    def z_copy(k):
        to = lax.rem(z + k, zs)
        return pltpu.make_async_remote_copy(
            src_ref=passed.at[to],
            dst_ref=far.at[k],
            send_sem=zsend.at[k],
            recv_sem=zrecv.at[k],
            device_id=(y * zs + to, slice_index),
            device_id_type=MESH,
        )

    def part_copy(k):
        return pltpu.make_async_remote_copy(
            src_ref=part,
            dst_ref=others.at[k],
            send_sem=psend.at[k],
            recv_sem=precv.at[k],
            device_id=(me, lax.rem(slice_index + k, slices)),
            device_id_type=MESH,
        )

    for k in range(1, ys):
        y_copy(k).start()
    list_squares(hot, squares, parts, total)
    for t in range(part.shape[0]):
        at = slice(t * LANES, (t + 1) * LANES)
        part[t : t + 1, :] = total[0:1, at] + total[1:2, at] + total[2:3, at]

    @pl.loop(1, slices)
    def _(k):
        part_copy(k).start()

    near[0] = share[y]
    for k in range(1, ys):
        y_copy(k).wait_recv()
    passed[...] = jnp.sum(near[...], axis=0)

    @pl.loop(1, zs)
    def _(k):
        z_copy(k).start()

    far[0] = passed[z]
    others[0] = part[...]

    @pl.loop(1, slices)
    def _(k):
        part_copy(k).wait_recv()

    spread = jnp.sum(others[...], axis=0)
    for t in range(part.shape[0]):
        error_ref[t : t + 1, :] = spread[t : t + 1, :] / (total[3:4, t * LANES : (t + 1) * LANES] + 1.0)

    @pl.loop(1, zs)
    def _(k):
        z_copy(k).wait_recv()

    whole = jnp.sum(far[...], axis=0)
    words_ref[...] = (whole[:mine] + prior * books_ref[...]) / (whole[mine:] + prior)

    for k in range(1, ys):
        y_copy(k).wait_send()

    @pl.loop(1, zs)
    def _(k):
        z_copy(k).wait_send()

    @pl.loop(1, slices)
    def _(k):
        part_copy(k).wait_send()


def main_kernel(
    subs, prior, from_ref, vec_ref, meta_ref, old_ref, books_ref, new_ref, error_ref, words_ref,
    rows, tmp, send, recv, acc, both, listcol, listrow, hot, resid, upper, squares, parts, total, c8,
    n8, sums, counts, share, near, passed, far, part, others,
    send_sem, recv_sem, ysend, yrecv, zsend, zrecv, psend, precv,
):
    owners, slots = from_ref.shape
    count = vec_ref.shape[0]
    slices = others.shape[0]
    mine = books_ref.shape[0]
    ys, zs = share.shape[0], share.shape[1]
    me, slice_index = lax.axis_index("rows"), lax.axis_index("dims")
    y, z = me // zs, lax.rem(me, zs)

    barrier = pltpu.get_barrier_semaphore()

    @pl.loop(1, owners)
    def _(k):
        pl.semaphore_signal(
            barrier, inc=1, device_id=(lax.rem(me + k, owners), slice_index), device_id_type=MESH
        )

    @pl.loop(1, slices)
    def _(k):
        pl.semaphore_signal(
            barrier, inc=1, device_id=(me, lax.rem(slice_index + k, slices)), device_id_type=MESH
        )

    rows[0:count, :] = vec_ref[...].astype(jnp.float32)
    rows[count:, :] = jnp.zeros((rows.shape[0] - count, LANES), jnp.float32)
    constants(listcol, listrow)
    acc[...] = jnp.zeros_like(acc)
    n8[...] = jnp.zeros_like(n8)
    pl.semaphore_wait(barrier, owners + slices - 2)

    def pack(d):
        @pl.loop(0, slots // 8)
        def _(q):
            for r in range(8):
                i = from_ref[d, q * 8 + r]
                tmp[pl.ds(q * 8 + r, 1), :] = rows[pl.ds(i, 1), :]

    def copy_to(k):
        d = lax.rem(me + k, owners)
        return pltpu.make_async_remote_copy(
            src_ref=send.at[k],
            dst_ref=recv.at[k],
            send_sem=send_sem.at[k],
            recv_sem=recv_sem.at[k],
            device_id=(d, slice_index),
            device_id_type=MESH,
        )

    @pl.loop(1, owners)
    def _(k):
        d = lax.rem(me + k, owners)
        pack(d)
        send[k, 0:slots, :] = tmp[...].astype(jnp.bfloat16)
        send[k, slots:, :] = meta_ref[d]
        copy_to(k).start()

    pack(me)
    recv[0, 0:slots, :] = tmp[...].astype(jnp.bfloat16)
    recv[0, slots:, :] = meta_ref[me]

    @pl.loop(0, owners // GROUP)
    def _(g):
        for j in range(GROUP):
            k = g * GROUP + j

            @pl.when(k > 0)
            def _():
                copy_to(k).wait_recv()

        absorb(g, subs, recv, acc, hot, listcol, listrow, upper, n8)

    finish(
        subs, prior, old_ref, books_ref, new_ref, error_ref, words_ref, recv, acc, both, hot, resid, upper, squares, parts,
        total, c8, n8, sums, counts, share, near, passed, far, part, others, ysend, yrecv, zsend, zrecv, psend, precv,
    )

    @pl.loop(1, owners)
    def _(k):
        copy_to(k).wait_send()


def fast_kernel(
    subs, prior, from_ref, spill_from_ref, vec_ref, meta_ref, spill_meta_ref, old_ref, books_ref,
    new_ref, error_ref, words_ref, flag_ref,
    rows, tmp, send, land, spills, recv, acc, both, listcol, listrow, hot, resid, upper, squares, parts, total, c8,
    n8, sums, counts, share, near, passed, far, part, others,
    send_sem, recv_sem, spill_recv, plus_send, minus_send, over_send, ysend, yrecv, zsend, zrecv, psend, precv,
):
    owners, slots = from_ref.shape
    count = vec_ref.shape[0]
    slices = others.shape[0]
    mine = books_ref.shape[0]
    ys, zs = share.shape[0], share.shape[1]
    me, slice_index = lax.axis_index("rows"), lax.axis_index("dims")
    y, z = me // zs, lax.rem(me, zs)

    barrier = pltpu.get_barrier_semaphore()

    @pl.loop(1, owners)
    def _(k):
        pl.semaphore_signal(
            barrier, inc=1, device_id=(lax.rem(me + k, owners), slice_index), device_id_type=MESH
        )

    @pl.loop(1, slices)
    def _(k):
        pl.semaphore_signal(
            barrier, inc=1, device_id=(me, lax.rem(slice_index + k, slices)), device_id_type=MESH
        )

    rows[0:count, :] = vec_ref[...].astype(jnp.float32)
    rows[count:, :] = jnp.zeros((rows.shape[0] - count, LANES), jnp.float32)
    constants(listcol, listrow)
    acc[...] = jnp.zeros_like(acc)
    n8[...] = jnp.zeros_like(n8)
    flag_ref[...] = jnp.zeros_like(flag_ref)
    pl.semaphore_wait(barrier, owners + slices - 2)

    def pack(source, row, height):
        @pl.loop(0, height // 8)
        def _(q):
            for r in range(8):
                i = source[row, q * 8 + r]
                tmp[pl.ds(q * 8 + r, 1), :] = rows[pl.ds(i, 1), :]

    def place(k, sign):
        u = k + ys
        j, r = u // (2 * ys), lax.rem(u, 2 * ys)
        dz, dy = jnp.where(r < ys, j, -j) * sign, lax.rem(r, ys) * sign
        return lax.rem(y + dy + ys, ys), lax.rem(z + dz + zs, zs)

    def copy_to(k):
        to_y, to_z = place(k, 1)
        d = to_y * zs + to_z
        return pltpu.make_async_remote_copy(
            src_ref=send.at[k],
            dst_ref=land.at[k],
            send_sem=send_sem.at[k],
            recv_sem=recv_sem.at[k],
            device_id=(d, slice_index),
            device_id_type=MESH,
        )

    def spill_copy(source_z, to_y, to_z, sem):
        return pltpu.make_async_remote_copy(
            src_ref=spills.at[y, source_z],
            dst_ref=spills.at[y, source_z],
            send_sem=sem,
            recv_sem=spill_recv.at[y, source_z],
            device_id=(to_y * zs + to_z, slice_index),
            device_id_type=MESH,
        )

    def arrived(source_y, source_z):
        pltpu.make_async_remote_copy(
            src_ref=spills.at[source_y, source_z],
            dst_ref=spills.at[source_y, source_z],
            send_sem=plus_send.at[0],
            recv_sem=spill_recv.at[source_y, source_z],
            device_id=(y * zs + lax.rem(z + 1, zs), slice_index),
            device_id_type=MESH,
        ).wait_recv()

    def pass_plus(j):
        return spill_copy(lax.rem(z - j + 1 + zs, zs), y, lax.rem(z + 1, zs), plus_send.at[j])

    def pass_minus(j):
        return spill_copy(lax.rem(z + j - 1, zs), y, lax.rem(z - 1 + zs, zs), minus_send.at[j])

    def pass_over(source_z, dy):
        return spill_copy(source_z, lax.rem(y + dy, ys), z, over_send.at[dy, source_z])

    def over(source_z):
        for dy in range(1, ys):
            pass_over(source_z, dy).start()

    pack(spill_from_ref, 0, SPILL)
    spills[y, z, 0:SPILL, :] = tmp[...].astype(jnp.bfloat16)
    spills[y, z, SPILL:, :] = spill_meta_ref[...]
    steps = zs // 2
    pass_plus(1).start()
    if steps > 1:
        pass_minus(1).start()
    over(z)
    def send_to(k):
        to_y, to_z = place(k, 1)
        d = to_y * zs + to_z
        pack(from_ref, d, NEAR)
        send[k, 0:NEAR, :] = tmp[0:NEAR, :].astype(jnp.bfloat16)
        send[k, NEAR:, :] = meta_ref[d]
        copy_to(k).start()

    def process(g):
        for i in range(GROUP):
            k = g * GROUP + i
            from_y, from_z = place(k, -1)

            @pl.when(k > 0)
            def _():
                copy_to(k).wait_recv()

            @pl.when(from_y != y)
            def _():
                arrived(from_y, from_z)

        for i in range(GROUP):
            k = g * GROUP + i
            from_y, from_z = place(k, -1)
            assemble(k, subs, land, spills.at[from_y, from_z], recv, flag_ref)
        absorb(g, subs, recv, acc, hot, listcol, listrow, upper, n8)

    pack(from_ref, me, NEAR)
    land[0, 0:NEAR, :] = tmp[0:NEAR, :].astype(jnp.bfloat16)
    land[0, NEAR:, :] = meta_ref[me]

    @pl.loop(1, ys)
    def _(k):
        send_to(k)

    ring = 2 * ys
    pieces = ring // GROUP

    @pl.loop(0, steps)
    def _(t):
        @pl.loop(0, ring)
        def _(q):
            k = ys + t * ring + q

            @pl.when(k < owners)
            def _():
                send_to(k)

        j = t + 1
        before = lax.rem(z - j + zs, zs)
        arrived(y, before)

        @pl.when(j < steps)
        def _():
            pass_plus(j + 1).start()

        over(before)

        @pl.when(j < steps)
        def _():
            after = lax.rem(z + j, zs)
            arrived(y, after)

            @pl.when(j < steps - 1)
            def _():
                pass_minus(j + 1).start()

            over(after)

        @pl.loop(0, pieces)
        def _(q):
            g = (t - 2) * pieces + q + 1

            @pl.when(g >= 0)
            def _():
                process(g)

    done = (steps - 2) * pieces + 1

    @pl.loop(max(done, 0), owners // GROUP)
    def _(g):
        process(g)

    finish(
        subs, prior, old_ref, books_ref, new_ref, error_ref, words_ref, recv, acc, both, hot, resid, upper, squares, parts,
        total, c8, n8, sums, counts, share, near, passed, far, part, others, ysend, yrecv, zsend, zrecv, psend, precv,
    )

    @pl.loop(1, owners)
    def _(k):
        copy_to(k).wait_send()

    @pl.loop(1, steps + 1)
    def _(j):
        pass_plus(j).wait_send()

    @pl.loop(1, steps)
    def _(j):
        pass_minus(j).wait_send()

    @pl.loop(0, zs)
    def _(source_z):
        for dy in range(1, ys):
            pass_over(source_z, dy).wait_send()


def vmem_spec():
    return pl.BlockSpec(memory_space=pltpu.VMEM)


def tail_scratch(owners, slots, owned, subs, codewords, mine, slices):
    f32, bf16 = jnp.float32, jnp.bfloat16
    vmem, dma = pltpu.VMEM, pltpu.SemaphoreType.DMA
    zs = owners // YS
    wide = min(2048, owners * slots)
    arrays = [
        vmem((owners, slots + META, LANES), bf16),
        vmem((owned, 2 * LANES), f32),
        vmem((owned, 2 * LANES), bf16),
        vmem((owned // 16, 16, LANES), bf16),
        vmem((owned // LANES, 16, LANES), bf16),
        vmem((owners * slots, owned), bf16),
        vmem((owners * slots, LANES), bf16),
        vmem((owners * slots, LANES), bf16),
        vmem((owners * slots, 2 * LANES), bf16),
        vmem((owners * slots // wide, 16, wide), bf16),
        vmem((16, owned), f32),
        vmem((subs, codewords // 2, 2 * LANES), f32),
        vmem((subs, codewords // 2, 2 * LANES), f32),
        vmem((codewords, LANES), f32),
        vmem((codewords, LANES), f32),
        vmem((YS, zs, 2 * mine, LANES), f32),
        vmem((YS, zs, 2 * mine, LANES), f32),
        vmem((zs, 2 * mine, LANES), f32),
        vmem((zs, 2 * mine, LANES), f32),
        vmem((owned // LANES, LANES), f32),
        vmem((slices, owned // LANES, LANES), f32),
    ]
    return arrays, [dma((YS,))] * 2 + [dma((zs,))] * 2 + [dma((slices,))] * 2


def body(vectors, list_ids, codes, old_centroids, old_codebooks):
    owners = lax.axis_size("rows")
    slices = lax.axis_size("dims")
    count = vectors.shape[0]
    owned = old_centroids.shape[0]
    subs = codes.shape[1]
    mine = old_codebooks.shape[0]
    codewords = mine * owners
    slots = 2 * count // owners
    spill = SPILL_META // META * LANES
    zs = owners // YS
    f32, bf16, i32 = jnp.float32, jnp.bfloat16, jnp.int32
    vmem, dma, smem = pltpu.VMEM, pltpu.SemaphoreType.DMA, pl.BlockSpec(memory_space=pltpu.SMEM)
    prior = count * owners // (16 * codewords) * 1.0
    arrays, semaphores = tail_scratch(owners, slots, owned, subs, codewords, mine, slices)
    outs = (
        jax.ShapeDtypeStruct((owned, LANES), f32),
        jax.ShapeDtypeStruct((owned // LANES, LANES), f32),
        jax.ShapeDtypeStruct((mine, LANES), f32),
    )
    id_row, code_rows = list_ids.reshape(1, count), codes.T

    def plan(kernel, more, name):
        shapes = (
            jax.ShapeDtypeStruct((owners, META, LANES), bf16),
            jax.ShapeDtypeStruct((owners, slots), i32),
        ) + more
        return pl.pallas_call(
            functools.partial(kernel, owned),
            out_shape=shapes,
            in_specs=[vmem_spec()] * 2,
            out_specs=(vmem_spec(),) * len(shapes),
            scratch_shapes=[vmem((owners, META, LANES), f32)],
            compiler_params=pltpu.CompilerParams(vmem_limit_bytes=VMEM_BYTES),
            name=name,
        )(id_row, code_rows)

    meta, source, spill_meta, spill_source = plan(
        split_plan_kernel,
        (jax.ShapeDtypeStruct((SPILL_META, LANES), bf16), jax.ShapeDtypeStruct((1, spill), i32)),
        "split_plan",
    )
    fresh, errors, books, flag = pl.pallas_call(
        functools.partial(fast_kernel, subs, prior),
        out_shape=outs + (jax.ShapeDtypeStruct((1, LANES), f32),),
        in_specs=[smem] * 2 + [vmem_spec()] * 5,
        out_specs=(vmem_spec(),) * 4,
        scratch_shapes=[
            vmem((count + 8, LANES), f32),
            vmem((SPILL, LANES), f32),
            vmem((owners, NEAR + META, LANES), bf16),
            vmem((owners, NEAR + META, LANES), bf16),
            vmem((YS, zs, SPILL + SPILL_META, LANES), bf16),
        ]
        + arrays
        + [
            dma((owners,)),
            dma((owners,)),
            dma((YS, zs)),
            dma((zs,)),
            dma((zs,)),
            dma((YS, zs)),
        ]
        + semaphores,
        compiler_params=pltpu.CompilerParams(
            collective_id=0, has_side_effects=True, vmem_limit_bytes=VMEM_BYTES
        ),
        name="fast",
    )(source, spill_source, vectors, meta, spill_meta, old_centroids, old_codebooks)

    def again():
        meta, source = plan(plan_kernel, (), "plan")
        return pl.pallas_call(
            functools.partial(main_kernel, subs, prior),
            out_shape=outs,
            in_specs=[smem] + [vmem_spec()] * 4,
            out_specs=(vmem_spec(),) * 3,
            scratch_shapes=[
                vmem((count + 8, LANES), f32),
                vmem((slots, LANES), f32),
                vmem((owners, slots + META, LANES), bf16),
            ]
            + arrays
            + [dma((owners,)), dma((owners,))]
            + semaphores,
            compiler_params=pltpu.CompilerParams(
                collective_id=1, has_side_effects=True, vmem_limit_bytes=VMEM_BYTES
            ),
            name="main",
        )(source, vectors, meta, old_centroids, old_codebooks)

    fresh, errors, books = lax.cond(flag[0, 0] > 0.0, again, lambda: (fresh, errors, books))
    return fresh, errors.reshape(owned), books


def solution(mesh):
    in_specs = (
        P("rows", "dims"),
        P("rows"),
        P("rows", "dims"),
        P("rows", "dims"),
        P("rows", "dims"),
    )
    out_specs = (P("rows", "dims"), P("rows"), P("rows", "dims"))
    return jax.shard_map(body, mesh=mesh, in_specs=in_specs, out_specs=out_specs, check_vma=False)
```

```python
import functools

import jax
import jax.numpy as jnp
from jax import lax
from jax.experimental import pallas as pl
from jax.experimental.pallas import tpu as pltpu
from jax.sharding import PartitionSpec as P

MESH = pl.DeviceIdType.MESH
LANES = 128
META = 16
VMEM_BYTES = 56 << 20
YS = 4
GROUP = 4
WIDE = 8
NEAR = 80
SPILL = 224
SPILL_META = 2 * META
CHUNK = 16
NN = (((1,), (0,)), ((), ()))
NT = (((1,), (1,)), ((), ()))


def dot(a, b, dims=NN):
    return lax.dot_general(a, b, dims, preferred_element_type=jnp.float32)


def id_value(local, bits=7):
    return ((1 << bits) + (local & ((1 << bits) - 1))) << (local >> bits)


def plan_kernel(owned, ids_ref, codes_ref, meta_ref, from_ref, wide):
    owners, slots = from_ref.shape
    count = ids_ref.shape[1]
    subs = codes_ref.shape[0]
    ids = ids_ref[...]
    shift = owned.bit_length() - 1
    owner = ids >> shift
    value = id_value(ids & (owned - 1)).astype(jnp.float32)
    mine = lax.broadcasted_iota(jnp.int32, (owners, count), 0) == owner
    hits = mine.astype(jnp.float32).astype(jnp.bfloat16)
    piece = min(512, count)
    before = (
        lax.broadcasted_iota(jnp.int32, (piece, piece), 0)
        < lax.broadcasted_iota(jnp.int32, (piece, piece), 1)
    ).astype(jnp.float32).astype(jnp.bfloat16)
    running = jnp.zeros((owners, 1), jnp.float32)
    ranks = []
    for c in range(count // piece):
        part = hits[:, c * piece : (c + 1) * piece]
        wide_part = part.astype(jnp.float32)
        earlier = dot(part, before) + running
        ranks.append(jnp.sum(earlier * wide_part, axis=0, keepdims=True))
        running = running + jnp.sum(wide_part, axis=1, keepdims=True)
    rank = jnp.concatenate(ranks, axis=1).astype(jnp.int32)
    placed = (lax.broadcasted_iota(jnp.int32, (slots, count), 0) == rank)
    placed = placed.astype(jnp.float32).astype(jnp.bfloat16)
    index = lax.broadcasted_iota(jnp.int32, (1, count), 1)

    def spread(row):
        return dot(jnp.where(mine, row, 0.0).astype(jnp.bfloat16), placed, NT)

    for m in range(subs):
        wide[:, m, :] = spread((codes_ref[m : m + 1, :] + 1).astype(jnp.float32))
    seen = spread(value)
    wide[:, subs, :] = seen
    for m in range(subs + 1, META):
        wide[:, m, :] = jnp.zeros((owners, slots), jnp.float32)
    high = spread((index >> 6).astype(jnp.float32))
    low = spread((index & 63).astype(jnp.float32))
    from_ref[...] = jnp.where(seen > 0.0, high * 64.0 + low, float(count)).astype(jnp.int32)
    meta_ref[...] = wide[...].astype(jnp.bfloat16)


def split_plan_kernel(owned, ids_ref, codes_ref, meta_ref, from_ref, spill_meta_ref, spill_from_ref, wide):
    owners, slots = from_ref.shape
    count = ids_ref.shape[1]
    subs = codes_ref.shape[0]
    spill = spill_from_ref.shape[1]
    ids = ids_ref[...]
    shift = owned.bit_length() - 1
    owner = ids >> shift
    value = id_value(ids & (owned - 1)).astype(jnp.float32)
    mine = lax.broadcasted_iota(jnp.int32, (owners, count), 0) == owner
    hits = mine.astype(jnp.float32).astype(jnp.bfloat16)
    piece = min(512, count)
    before = (
        lax.broadcasted_iota(jnp.int32, (piece, piece), 0)
        < lax.broadcasted_iota(jnp.int32, (piece, piece), 1)
    ).astype(jnp.float32).astype(jnp.bfloat16)
    running = jnp.zeros((owners, 1), jnp.float32)
    ranks = []
    for c in range(count // piece):
        part = hits[:, c * piece : (c + 1) * piece]
        wide_part = part.astype(jnp.float32)
        earlier = dot(part, before) + running
        ranks.append(jnp.sum(earlier * wide_part, axis=0, keepdims=True))
        running = running + jnp.sum(wide_part, axis=1, keepdims=True)
    rank = jnp.concatenate(ranks, axis=1)
    beyond = jnp.broadcast_to(jnp.maximum(running - NEAR, 0.0), (owners, LANES))
    lower = (
        lax.broadcasted_iota(jnp.int32, (owners, owners), 0)
        > lax.broadcasted_iota(jnp.int32, (owners, owners), 1)
    ).astype(jnp.float32).astype(jnp.bfloat16)
    start = dot(lower, beyond.astype(jnp.bfloat16))
    total = jnp.sum(beyond, axis=0, keepdims=True)
    first = jnp.sum(jnp.where(mine, start[:, 0:1], 0.0), axis=0, keepdims=True)
    near = jnp.where(rank < NEAR, rank, -1.0).astype(jnp.int32)
    far = jnp.where(rank < NEAR, -1.0, first + rank - NEAR).astype(jnp.int32)
    placed = lax.broadcasted_iota(jnp.int32, (slots, count), 0) == near
    placed = placed.astype(jnp.float32).astype(jnp.bfloat16)
    spilled = lax.broadcasted_iota(jnp.int32, (spill, count), 0) == far
    spilled = spilled.astype(jnp.float32).astype(jnp.bfloat16)
    index = lax.broadcasted_iota(jnp.int32, (1, count), 1)
    upper_index = (index >> 6).astype(jnp.float32)
    lower_index = (index & 63).astype(jnp.float32)
    words = (codes_ref[...] + 1).astype(jnp.float32)

    values = [words[m : m + 1, :] for m in range(subs)] + [value, upper_index, lower_index]
    given = jnp.concatenate([jnp.where(mine, row, 0.0).astype(jnp.bfloat16) for row in values], axis=0)
    given = dot(given, placed, NT)
    given = [given[m * owners : (m + 1) * owners, :] for m in range(len(values))]
    for m in range(subs + 1):
        wide[:, m, :] = given[m]
    wide[:, subs + 1, :] = start
    wide[:, subs + 2, :] = start + beyond
    wide[:, subs + 3, :] = jnp.broadcast_to(jnp.where(total > SPILL, 1.0, 0.0), (owners, LANES))
    for m in range(subs + 4, META):
        wide[:, m, :] = jnp.zeros((owners, slots), jnp.float32)
    seen, high, low = given[subs:]
    from_ref[...] = jnp.where(seen > 0.0, high * 64.0 + low, float(count)).astype(jnp.int32)
    meta_ref[...] = wide[...].astype(jnp.bfloat16)
    row = lax.broadcasted_iota(jnp.int32, (META - subs, count), 0)
    more = jnp.where(row == 0, value, jnp.where(row == 1, upper_index, jnp.where(row == 2, lower_index, 0.0)))
    moved = dot(jnp.concatenate([words, more], axis=0).astype(jnp.bfloat16), spilled, NT)
    spill_from_ref[...] = jnp.where(
        moved[subs : subs + 1] > 0.0,
        moved[subs + 1 : subs + 2] * 64.0 + moved[subs + 2 : subs + 3],
        float(count),
    ).astype(jnp.int32)
    for t in range(spill // LANES):
        spill_meta_ref[t * META : (t + 1) * META, :] = moved[:, t * LANES : (t + 1) * LANES].astype(jnp.bfloat16)


def constants(listcol, listrow):
    groups, lists = listcol.shape[0], listrow.shape[0]
    at = lax.broadcasted_iota(jnp.int32, (groups, 16, LANES), 0) * 16
    at = at + lax.broadcasted_iota(jnp.int32, (groups, 16, LANES), 1)
    listcol[...] = id_value(at).astype(jnp.float32).astype(jnp.bfloat16)
    at = lax.broadcasted_iota(jnp.int32, (lists, 16, LANES), 0) * LANES
    at = at + lax.broadcasted_iota(jnp.int32, (lists, 16, LANES), 2)
    listrow[...] = id_value(at).astype(jnp.float32).astype(jnp.bfloat16)


def one_hot(hit):
    made = jnp.where(hit, jnp.bfloat16(1), jnp.bfloat16(0))
    return made.reshape(made.shape[0] * made.shape[1], made.shape[2])


def low_words(v):
    return v - jnp.where(v > 128.5, 128.0, 0.0)


def word_rows(count):
    words = lax.broadcasted_iota(jnp.int32, (count // 16, 16, LANES), 0) * 16
    words = words + lax.broadcasted_iota(jnp.int32, (count // 16, 16, LANES), 1) + 1
    return words.astype(jnp.float32).astype(jnp.bfloat16)


def absorb(g, subs, recv, acc, hot, listcol, listrow, upper, n8):
    slots = recv.shape[1] - META
    lists = listrow.shape[0]
    hots, xs = [], []
    ones = jnp.ones((slots, LANES), jnp.bfloat16)
    words = word_rows(n8.shape[1])
    metas = [recv[g * GROUP + j, slots:, :].astype(jnp.float32) for j in range(GROUP)]
    uppers = []
    for j in range(GROUP):
        b = g * GROUP + j
        v = metas[j][subs : subs + 1, :]
        row = jnp.broadcast_to(v, (16, LANES)).astype(jnp.bfloat16)
        hots.append(one_hot(listcol[...] == row[None]))
        xs.append(jnp.concatenate([recv[b, 0:slots, :], ones], axis=1))
        column = jnp.broadcast_to(v, (slots, LANES)).T.astype(jnp.bfloat16)
        column = column.reshape(slots // 16, 16, LANES)
        start = pl.multiple_of(b * slots, slots)
        for t in range(lists):
            hot[pl.ds(start, slots), t * LANES : (t + 1) * LANES] = one_hot(column == listrow[t][None])
        is_upper = jnp.where(metas[j] > 128.5, 1.0, 0.0)
        is_upper = jnp.concatenate(
            [jnp.broadcast_to(is_upper[m : m + 1, :], (LANES // subs, LANES)) for m in range(subs)], axis=0
        )
        is_upper = is_upper.T.astype(jnp.bfloat16)
        upper[pl.ds(start, slots), :] = is_upper
        uppers.append(jnp.concatenate([ones - is_upper, is_upper], axis=1))
    acc[...] += dot(jnp.concatenate(hots, axis=1), jnp.concatenate(xs, axis=0))
    halves = jnp.concatenate(uppers, axis=0)
    lows = [low_words(v) for v in metas]
    for m in range(subs):
        hots = []
        for j in range(GROUP):
            row = jnp.broadcast_to(lows[j][m : m + 1, :], (16, LANES)).astype(jnp.bfloat16)
            hots.append(one_hot(words == row[None]))
        n8[m] += dot(jnp.concatenate(hots, axis=1), halves)


def refit(old_ref, new_ref, acc, both):
    fresh = (acc[:, :LANES] + old_ref[...]) / (acc[:, LANES:] + 1.0)
    new_ref[...] = fresh
    top = fresh.astype(jnp.bfloat16)
    both[:, :LANES] = top
    both[:, LANES:] = (fresh - top.astype(jnp.float32)).astype(jnp.bfloat16)


def residuals(recv, hot, both, resid, squares):
    owners, slots = recv.shape[0], recv.shape[1] - META
    per = min(WIDE, owners)
    wide = per * slots

    @pl.loop(0, owners // per)
    def _(g):
        start = pl.multiple_of(g * wide, wide)
        looked = dot(hot[pl.ds(start, wide), :], both[...])
        x = jnp.concatenate([recv[g * per + j, 0:slots, :] for j in range(per)], axis=0)
        diff = x.astype(jnp.float32) - (looked[:, :LANES] + looked[:, LANES:])
        resid[pl.ds(start, wide), :] = diff.astype(jnp.bfloat16)
        square = diff * diff
        top = square.astype(jnp.bfloat16)
        squares[pl.ds(start, wide), :LANES] = top
        squares[pl.ds(start, wide), LANES:] = (square - top.astype(jnp.float32)).astype(jnp.bfloat16)


def code_sums(subs, recv, resid, upper, c8):
    owners, slots = recv.shape[0], recv.shape[1] - META
    per = min(CHUNK, owners)
    words = word_rows(c8.shape[1])
    c8[...] = jnp.zeros_like(c8)

    @pl.loop(0, owners // per)
    def _(g):
        start = pl.multiple_of(g * per * slots, per * slots)
        r = resid[pl.ds(start, per * slots), :]
        in_upper = r * upper[pl.ds(start, per * slots), :]
        right = jnp.concatenate([r - in_upper, in_upper], axis=1)
        lows = [low_words(recv[g * per + j, slots:, :].astype(jnp.float32)) for j in range(per)]
        for m in range(subs):
            hots = []
            for j in range(per):
                row = jnp.broadcast_to(lows[j][m : m + 1, :], (16, LANES)).astype(jnp.bfloat16)
                hots.append(one_hot(words == row[None]))
            c8[m] += dot(jnp.concatenate(hots, axis=1), right)


def list_squares(hot, squares, parts, total):
    count = squares.shape[0]
    wide = min(2048, count)
    ones = jnp.ones((16, 2 * LANES), jnp.bfloat16)
    kind = lax.broadcasted_iota(jnp.int32, (16, wide), 0)

    @pl.loop(0, count // wide)
    def _(g):
        start = pl.multiple_of(g * wide, wide)
        row = dot(ones, squares[pl.ds(start, wide), :], NT)
        first = row.astype(jnp.bfloat16).astype(jnp.float32)
        second = (row - first).astype(jnp.bfloat16).astype(jnp.float32)
        third = row - first - second
        row = jnp.where(kind == 0, first, jnp.where(kind == 1, second, jnp.where(kind == 2, third, 1.0)))
        parts[g] = row.astype(jnp.bfloat16)

    total[...] = jnp.zeros_like(total)

    @pl.loop(0, count // wide)
    def _(g):
        start = pl.multiple_of(g * wide, wide)
        total[...] += dot(parts[g], hot[pl.ds(start, wide), :])


def gather_shares(subs, mine, c8, n8, sums, counts, share):
    half = c8.shape[1]
    codewords = 2 * half
    sub = lax.broadcasted_iota(jnp.int32, (half, LANES), 1) // (LANES // subs)
    for taken, given in ((c8, sums), (n8, counts)):
        for h in range(2):
            s = jnp.zeros((half, LANES), jnp.float32)
            for m in range(subs):
                s = jnp.where(sub == m, taken[m, :, h * LANES : (h + 1) * LANES], s)
            given[h * half : (h + 1) * half, :] = s
    for d in range(codewords // mine):
        share[d // share.shape[1], d % share.shape[1], 0:mine, :] = sums[d * mine : (d + 1) * mine, :]
        share[d // share.shape[1], d % share.shape[1], mine:, :] = counts[d * mine : (d + 1) * mine, :]


def assemble(b, subs, land, block, recv, flag):
    slots = recv.shape[1] - META
    meta = land[b, NEAR:, :].astype(jnp.float32)
    begin, end = meta[subs + 1 : subs + 2, :], meta[subs + 2 : subs + 3, :]
    flag[...] = jnp.maximum(flag[...], meta[subs + 3 : subs + 4, :])
    slot = lax.broadcasted_iota(jnp.int32, (slots, LANES), 0)
    lane = lax.broadcasted_iota(jnp.int32, (slots, LANES), 1)
    halves = []
    for t in range(SPILL_META // META):
        at = (lane + t * LANES).astype(jnp.float32)
        wanted = jnp.where(slot >= NEAR, lane + t * LANES + NEAR - slot, -1).astype(jnp.float32)
        hit = jnp.logical_and(wanted == begin, at < end)
        halves.append(jnp.where(hit, 1.0, 0.0))
    pick = jnp.concatenate(halves, axis=1).astype(jnp.bfloat16)
    taken = dot(pick, block[...])
    recv[b, 0:NEAR, :] = land[b, 0:NEAR, :]
    recv[b, NEAR:slots, :] = taken[NEAR:, :].astype(jnp.bfloat16)
    labels = jnp.concatenate(
        [block[SPILL + t * META : SPILL + (t + 1) * META, :] for t in range(SPILL_META // META)], axis=1
    )
    keep = lax.broadcasted_iota(jnp.int32, (META, LANES), 1) < NEAR
    recv[b, slots:, :] = jnp.where(keep, meta, dot(labels, pick, NT)).astype(jnp.bfloat16)


def finish(
    subs, prior, old_ref, books_ref, new_ref, error_ref, words_ref, recv, acc, both, hot, resid, upper, squares, parts,
    total, c8, n8, sums, counts, share, near, passed, far, part, others, ysend, yrecv, zsend, zrecv, psend, precv,
):
    slices, mine = others.shape[0], books_ref.shape[0]
    ys, zs = share.shape[0], share.shape[1]
    me, slice_index = lax.axis_index("rows"), lax.axis_index("dims")
    y, z = me // zs, lax.rem(me, zs)
    refit(old_ref, new_ref, acc, both)
    residuals(recv, hot, both, resid, squares)
    code_sums(subs, recv, resid, upper, c8)
    gather_shares(subs, mine, c8, n8, sums, counts, share)

    def y_copy(k):
        to = lax.rem(y + k, ys)
        return pltpu.make_async_remote_copy(
            src_ref=share.at[to],
            dst_ref=near.at[k],
            send_sem=ysend.at[k],
            recv_sem=yrecv.at[k],
            device_id=(to * zs + z, slice_index),
            device_id_type=MESH,
        )

    def z_copy(k):
        to = lax.rem(z + k, zs)
        return pltpu.make_async_remote_copy(
            src_ref=passed.at[to],
            dst_ref=far.at[k],
            send_sem=zsend.at[k],
            recv_sem=zrecv.at[k],
            device_id=(y * zs + to, slice_index),
            device_id_type=MESH,
        )

    def part_copy(k):
        return pltpu.make_async_remote_copy(
            src_ref=part,
            dst_ref=others.at[k],
            send_sem=psend.at[k],
            recv_sem=precv.at[k],
            device_id=(me, lax.rem(slice_index + k, slices)),
            device_id_type=MESH,
        )

    for k in range(1, ys):
        y_copy(k).start()
    list_squares(hot, squares, parts, total)
    for t in range(part.shape[0]):
        at = slice(t * LANES, (t + 1) * LANES)
        part[t : t + 1, :] = total[0:1, at] + total[1:2, at] + total[2:3, at]

    @pl.loop(1, slices)
    def _(k):
        part_copy(k).start()

    near[0] = share[y]
    for k in range(1, ys):
        y_copy(k).wait_recv()
    passed[...] = jnp.sum(near[...], axis=0)

    @pl.loop(1, zs)
    def _(k):
        z_copy(k).start()

    far[0] = passed[z]
    others[0] = part[...]

    @pl.loop(1, slices)
    def _(k):
        part_copy(k).wait_recv()

    spread = jnp.sum(others[...], axis=0)
    for t in range(part.shape[0]):
        error_ref[t : t + 1, :] = spread[t : t + 1, :] / (total[3:4, t * LANES : (t + 1) * LANES] + 1.0)

    @pl.loop(1, zs)
    def _(k):
        z_copy(k).wait_recv()

    whole = jnp.sum(far[...], axis=0)
    words_ref[...] = (whole[:mine] + prior * books_ref[...]) / (whole[mine:] + prior)

    for k in range(1, ys):
        y_copy(k).wait_send()

    @pl.loop(1, zs)
    def _(k):
        z_copy(k).wait_send()

    @pl.loop(1, slices)
    def _(k):
        part_copy(k).wait_send()


def main_kernel(
    subs, prior, from_ref, vec_ref, meta_ref, old_ref, books_ref, new_ref, error_ref, words_ref,
    rows, tmp, send, recv, acc, both, listcol, listrow, hot, resid, upper, squares, parts, total, c8,
    n8, sums, counts, share, near, passed, far, part, others,
    send_sem, recv_sem, ysend, yrecv, zsend, zrecv, psend, precv,
):
    owners, slots = from_ref.shape
    count = vec_ref.shape[0]
    slices = others.shape[0]
    mine = books_ref.shape[0]
    ys, zs = share.shape[0], share.shape[1]
    me, slice_index = lax.axis_index("rows"), lax.axis_index("dims")
    y, z = me // zs, lax.rem(me, zs)

    barrier = pltpu.get_barrier_semaphore()

    @pl.loop(1, owners)
    def _(k):
        pl.semaphore_signal(
            barrier, inc=1, device_id=(lax.rem(me + k, owners), slice_index), device_id_type=MESH
        )

    @pl.loop(1, slices)
    def _(k):
        pl.semaphore_signal(
            barrier, inc=1, device_id=(me, lax.rem(slice_index + k, slices)), device_id_type=MESH
        )

    rows[0:count, :] = vec_ref[...].astype(jnp.float32)
    rows[count:, :] = jnp.zeros((rows.shape[0] - count, LANES), jnp.float32)
    constants(listcol, listrow)
    acc[...] = jnp.zeros_like(acc)
    n8[...] = jnp.zeros_like(n8)
    pl.semaphore_wait(barrier, owners + slices - 2)

    def pack(d):
        @pl.loop(0, slots // 8)
        def _(q):
            for r in range(8):
                i = from_ref[d, q * 8 + r]
                tmp[pl.ds(q * 8 + r, 1), :] = rows[pl.ds(i, 1), :]

    def copy_to(k):
        d = lax.rem(me + k, owners)
        return pltpu.make_async_remote_copy(
            src_ref=send.at[k],
            dst_ref=recv.at[k],
            send_sem=send_sem.at[k],
            recv_sem=recv_sem.at[k],
            device_id=(d, slice_index),
            device_id_type=MESH,
        )

    @pl.loop(1, owners)
    def _(k):
        d = lax.rem(me + k, owners)
        pack(d)
        send[k, 0:slots, :] = tmp[...].astype(jnp.bfloat16)
        send[k, slots:, :] = meta_ref[d]
        copy_to(k).start()

    pack(me)
    recv[0, 0:slots, :] = tmp[...].astype(jnp.bfloat16)
    recv[0, slots:, :] = meta_ref[me]

    @pl.loop(0, owners // GROUP)
    def _(g):
        for j in range(GROUP):
            k = g * GROUP + j

            @pl.when(k > 0)
            def _():
                copy_to(k).wait_recv()

        absorb(g, subs, recv, acc, hot, listcol, listrow, upper, n8)

    finish(
        subs, prior, old_ref, books_ref, new_ref, error_ref, words_ref, recv, acc, both, hot, resid, upper, squares, parts,
        total, c8, n8, sums, counts, share, near, passed, far, part, others, ysend, yrecv, zsend, zrecv, psend, precv,
    )

    @pl.loop(1, owners)
    def _(k):
        copy_to(k).wait_send()


def fast_kernel(
    subs, prior, from_ref, spill_from_ref, vec_ref, meta_ref, spill_meta_ref, old_ref, books_ref,
    new_ref, error_ref, words_ref, flag_ref,
    rows, tmp, send, land, spills, recv, acc, both, listcol, listrow, hot, resid, upper, squares, parts, total, c8,
    n8, sums, counts, share, near, passed, far, part, others,
    send_sem, recv_sem, spill_recv, plus_send, minus_send, over_send, ysend, yrecv, zsend, zrecv, psend, precv,
):
    owners, slots = from_ref.shape
    count = vec_ref.shape[0]
    slices = others.shape[0]
    mine = books_ref.shape[0]
    ys, zs = share.shape[0], share.shape[1]
    me, slice_index = lax.axis_index("rows"), lax.axis_index("dims")
    y, z = me // zs, lax.rem(me, zs)

    barrier = pltpu.get_barrier_semaphore()

    @pl.loop(1, owners)
    def _(k):
        pl.semaphore_signal(
            barrier, inc=1, device_id=(lax.rem(me + k, owners), slice_index), device_id_type=MESH
        )

    @pl.loop(1, slices)
    def _(k):
        pl.semaphore_signal(
            barrier, inc=1, device_id=(me, lax.rem(slice_index + k, slices)), device_id_type=MESH
        )

    rows[0:count, :] = vec_ref[...].astype(jnp.float32)
    rows[count:, :] = jnp.zeros((rows.shape[0] - count, LANES), jnp.float32)
    constants(listcol, listrow)
    acc[...] = jnp.zeros_like(acc)
    n8[...] = jnp.zeros_like(n8)
    flag_ref[...] = jnp.zeros_like(flag_ref)
    pl.semaphore_wait(barrier, owners + slices - 2)

    def pack(source, row, height):
        @pl.loop(0, height // 8)
        def _(q):
            for r in range(8):
                i = source[row, q * 8 + r]
                tmp[pl.ds(q * 8 + r, 1), :] = rows[pl.ds(i, 1), :]

    def place(k, sign):
        u = k + ys
        j, r = u // (2 * ys), lax.rem(u, 2 * ys)
        dz, dy = jnp.where(r < ys, j, -j) * sign, lax.rem(r, ys) * sign
        return lax.rem(y + dy + ys, ys), lax.rem(z + dz + zs, zs)

    def copy_to(k):
        to_y, to_z = place(k, 1)
        d = to_y * zs + to_z
        return pltpu.make_async_remote_copy(
            src_ref=send.at[k],
            dst_ref=land.at[k],
            send_sem=send_sem.at[k],
            recv_sem=recv_sem.at[k],
            device_id=(d, slice_index),
            device_id_type=MESH,
        )

    def spill_copy(source_z, to_y, to_z, sem):
        return pltpu.make_async_remote_copy(
            src_ref=spills.at[y, source_z],
            dst_ref=spills.at[y, source_z],
            send_sem=sem,
            recv_sem=spill_recv.at[y, source_z],
            device_id=(to_y * zs + to_z, slice_index),
            device_id_type=MESH,
        )

    def arrived(source_y, source_z):
        pltpu.make_async_remote_copy(
            src_ref=spills.at[source_y, source_z],
            dst_ref=spills.at[source_y, source_z],
            send_sem=plus_send.at[0],
            recv_sem=spill_recv.at[source_y, source_z],
            device_id=(y * zs + lax.rem(z + 1, zs), slice_index),
            device_id_type=MESH,
        ).wait_recv()

    def pass_plus(j):
        return spill_copy(lax.rem(z - j + 1 + zs, zs), y, lax.rem(z + 1, zs), plus_send.at[j])

    def pass_minus(j):
        return spill_copy(lax.rem(z + j - 1, zs), y, lax.rem(z - 1 + zs, zs), minus_send.at[j])

    def pass_over(source_z, dy):
        return spill_copy(source_z, lax.rem(y + dy, ys), z, over_send.at[dy, source_z])

    def over(source_z):
        for dy in range(1, ys):
            pass_over(source_z, dy).start()

    pack(spill_from_ref, 0, SPILL)
    spills[y, z, 0:SPILL, :] = tmp[...].astype(jnp.bfloat16)
    spills[y, z, SPILL:, :] = spill_meta_ref[...]
    steps = zs // 2
    pass_plus(1).start()
    if steps > 1:
        pass_minus(1).start()
    over(z)
    def send_to(k):
        to_y, to_z = place(k, 1)
        d = to_y * zs + to_z
        pack(from_ref, d, NEAR)
        send[k, 0:NEAR, :] = tmp[0:NEAR, :].astype(jnp.bfloat16)
        send[k, NEAR:, :] = meta_ref[d]
        copy_to(k).start()

    def process(g):
        for i in range(GROUP):
            k = g * GROUP + i
            from_y, from_z = place(k, -1)

            @pl.when(k > 0)
            def _():
                copy_to(k).wait_recv()

            @pl.when(from_y != y)
            def _():
                arrived(from_y, from_z)

        for i in range(GROUP):
            k = g * GROUP + i
            from_y, from_z = place(k, -1)
            assemble(k, subs, land, spills.at[from_y, from_z], recv, flag_ref)
        absorb(g, subs, recv, acc, hot, listcol, listrow, upper, n8)

    pack(from_ref, me, NEAR)
    land[0, 0:NEAR, :] = tmp[0:NEAR, :].astype(jnp.bfloat16)
    land[0, NEAR:, :] = meta_ref[me]

    ring = 2 * ys

    @pl.loop(1, ys + ring)
    def _(k):
        send_to(k)

    pieces = ring // GROUP

    @pl.loop(0, steps)
    def _(t):
        @pl.loop(0, ring)
        def _(q):
            k = ys + (t + 1) * ring + q

            @pl.when(k < owners)
            def _():
                send_to(k)

        j = t + 1
        before = lax.rem(z - j + zs, zs)
        arrived(y, before)

        @pl.when(j < steps)
        def _():
            pass_plus(j + 1).start()

        over(before)

        @pl.when(j < steps)
        def _():
            after = lax.rem(z + j, zs)
            arrived(y, after)

            @pl.when(j < steps - 1)
            def _():
                pass_minus(j + 1).start()

            over(after)

        @pl.loop(0, pieces)
        def _(q):
            g = (t - 1) * pieces + q + 1

            @pl.when(g >= 0)
            def _():
                process(g)

    done = (steps - 1) * pieces + 1

    @pl.loop(max(done, 0), owners // GROUP)
    def _(g):
        process(g)

    finish(
        subs, prior, old_ref, books_ref, new_ref, error_ref, words_ref, recv, acc, both, hot, resid, upper, squares, parts,
        total, c8, n8, sums, counts, share, near, passed, far, part, others, ysend, yrecv, zsend, zrecv, psend, precv,
    )

    @pl.loop(1, owners)
    def _(k):
        copy_to(k).wait_send()

    @pl.loop(1, steps + 1)
    def _(j):
        pass_plus(j).wait_send()

    @pl.loop(1, steps)
    def _(j):
        pass_minus(j).wait_send()

    @pl.loop(0, zs)
    def _(source_z):
        for dy in range(1, ys):
            pass_over(source_z, dy).wait_send()


def vmem_spec():
    return pl.BlockSpec(memory_space=pltpu.VMEM)


def tail_scratch(owners, slots, owned, subs, codewords, mine, slices):
    f32, bf16 = jnp.float32, jnp.bfloat16
    vmem, dma = pltpu.VMEM, pltpu.SemaphoreType.DMA
    zs = owners // YS
    wide = min(2048, owners * slots)
    arrays = [
        vmem((owners, slots + META, LANES), bf16),
        vmem((owned, 2 * LANES), f32),
        vmem((owned, 2 * LANES), bf16),
        vmem((owned // 16, 16, LANES), bf16),
        vmem((owned // LANES, 16, LANES), bf16),
        vmem((owners * slots, owned), bf16),
        vmem((owners * slots, LANES), bf16),
        vmem((owners * slots, LANES), bf16),
        vmem((owners * slots, 2 * LANES), bf16),
        vmem((owners * slots // wide, 16, wide), bf16),
        vmem((16, owned), f32),
        vmem((subs, codewords // 2, 2 * LANES), f32),
        vmem((subs, codewords // 2, 2 * LANES), f32),
        vmem((codewords, LANES), f32),
        vmem((codewords, LANES), f32),
        vmem((YS, zs, 2 * mine, LANES), f32),
        vmem((YS, zs, 2 * mine, LANES), f32),
        vmem((zs, 2 * mine, LANES), f32),
        vmem((zs, 2 * mine, LANES), f32),
        vmem((owned // LANES, LANES), f32),
        vmem((slices, owned // LANES, LANES), f32),
    ]
    return arrays, [dma((YS,))] * 2 + [dma((zs,))] * 2 + [dma((slices,))] * 2


def body(vectors, list_ids, codes, old_centroids, old_codebooks):
    owners = lax.axis_size("rows")
    slices = lax.axis_size("dims")
    count = vectors.shape[0]
    owned = old_centroids.shape[0]
    subs = codes.shape[1]
    mine = old_codebooks.shape[0]
    codewords = mine * owners
    slots = 2 * count // owners
    spill = SPILL_META // META * LANES
    zs = owners // YS
    f32, bf16, i32 = jnp.float32, jnp.bfloat16, jnp.int32
    vmem, dma, smem = pltpu.VMEM, pltpu.SemaphoreType.DMA, pl.BlockSpec(memory_space=pltpu.SMEM)
    prior = count * owners // (16 * codewords) * 1.0
    arrays, semaphores = tail_scratch(owners, slots, owned, subs, codewords, mine, slices)
    outs = (
        jax.ShapeDtypeStruct((owned, LANES), f32),
        jax.ShapeDtypeStruct((owned // LANES, LANES), f32),
        jax.ShapeDtypeStruct((mine, LANES), f32),
    )
    id_row, code_rows = list_ids.reshape(1, count), codes.T

    def plan(kernel, more, name):
        shapes = (
            jax.ShapeDtypeStruct((owners, META, LANES), bf16),
            jax.ShapeDtypeStruct((owners, slots), i32),
        ) + more
        return pl.pallas_call(
            functools.partial(kernel, owned),
            out_shape=shapes,
            in_specs=[vmem_spec()] * 2,
            out_specs=(vmem_spec(),) * len(shapes),
            scratch_shapes=[vmem((owners, META, LANES), f32)],
            compiler_params=pltpu.CompilerParams(vmem_limit_bytes=VMEM_BYTES),
            name=name,
        )(id_row, code_rows)

    meta, source, spill_meta, spill_source = plan(
        split_plan_kernel,
        (jax.ShapeDtypeStruct((SPILL_META, LANES), bf16), jax.ShapeDtypeStruct((1, spill), i32)),
        "split_plan",
    )
    fresh, errors, books, flag = pl.pallas_call(
        functools.partial(fast_kernel, subs, prior),
        out_shape=outs + (jax.ShapeDtypeStruct((1, LANES), f32),),
        in_specs=[smem] * 2 + [vmem_spec()] * 5,
        out_specs=(vmem_spec(),) * 4,
        scratch_shapes=[
            vmem((count + 8, LANES), f32),
            vmem((SPILL, LANES), f32),
            vmem((owners, NEAR + META, LANES), bf16),
            vmem((owners, NEAR + META, LANES), bf16),
            vmem((YS, zs, SPILL + SPILL_META, LANES), bf16),
        ]
        + arrays
        + [
            dma((owners,)),
            dma((owners,)),
            dma((YS, zs)),
            dma((zs,)),
            dma((zs,)),
            dma((YS, zs)),
        ]
        + semaphores,
        compiler_params=pltpu.CompilerParams(
            collective_id=0, has_side_effects=True, vmem_limit_bytes=VMEM_BYTES
        ),
        name="fast",
    )(source, spill_source, vectors, meta, spill_meta, old_centroids, old_codebooks)

    def again():
        meta, source = plan(plan_kernel, (), "plan")
        return pl.pallas_call(
            functools.partial(main_kernel, subs, prior),
            out_shape=outs,
            in_specs=[smem] + [vmem_spec()] * 4,
            out_specs=(vmem_spec(),) * 3,
            scratch_shapes=[
                vmem((count + 8, LANES), f32),
                vmem((slots, LANES), f32),
                vmem((owners, slots + META, LANES), bf16),
            ]
            + arrays
            + [dma((owners,)), dma((owners,))]
            + semaphores,
            compiler_params=pltpu.CompilerParams(
                collective_id=1, has_side_effects=True, vmem_limit_bytes=VMEM_BYTES
            ),
            name="main",
        )(source, vectors, meta, old_centroids, old_codebooks)

    fresh, errors, books = lax.cond(flag[0, 0] > 0.0, again, lambda: (fresh, errors, books))
    return fresh, errors.reshape(owned), books


def solution(mesh):
    in_specs = (
        P("rows", "dims"),
        P("rows"),
        P("rows", "dims"),
        P("rows", "dims"),
        P("rows", "dims"),
    )
    out_specs = (P("rows", "dims"), P("rows"), P("rows", "dims"))
    return jax.shard_map(body, mesh=mesh, in_specs=in_specs, out_specs=out_specs, check_vma=False)
```
